32 devices in a mesh: geom: 2 (over x), row: 8 (over z, y), col: 2 (over core).
Axes of the slice: x: 2, y: 2, z: 4, core: 2. Of those that a mesh axis runs over, the one named last changes fastest.
Arguments:
- matrix: bfloat16 [128, 8, 128, 128], P(('geom', 'row'), 'col'), parts along dimension 0, may hold values from -1.5 to 1.5
- columns: int32 [64, 8], P('row'), may hold values from -1 to 63, as said below
Outputs:
- purified: bfloat16 [128, 8, 128, 128], P(('geom', 'row'), 'col'), parts along dimension 0
The draws below stay inside these ranges and needn't reach their ends.
There are 2 independent parts, one for each index of `geom`. The reference program is written for one: setup_inputs(seed, part) draws one part's arguments, and reference() takes and returns one part's arrays. A program takes and returns all parts, laid end to end along the dimension named above; an argument that names none is the same for every part. Nothing has to cross between parts.
Inputs may be any that keep to these rules, and one draw needn't show every extreme that they name: In block row i the valid slots come first and slot 0 holds i; valid slots hold distinct columns (i + d) mod 64 with -4 <= d <= 4, and the others hold -1. A block row has 1 to 8 valid slots, and some block row has 8.
All inputs are finite; a program needn't handle non-finite values.
Results may differ from the reference program's by a relative error of at most 0.0049.
Values may be sent and summed in bfloat16 or wider, within the bound.
No kernel may reach another device: no remote copies, remote signals or barrier semaphores. Data moves between devices by JAX's collectives and lax.ppermute only.
A program may use at most 64 MiB of HBM per device.

```python
import jax
import jax.numpy as jnp
from jax import lax

BS = 128
K = 8
BR_DEV = 8
REACH = 4
NB = 64


def draw_columns(key, part):
    window_span = 2 * REACH
    row_keys = jax.random.split(jax.random.fold_in(key, 11), NB)

    def one_row(row_key):
        shuffled = jax.random.permutation(row_key, window_span)
        return jnp.where(shuffled < REACH, shuffled - REACH, shuffled - REACH + 1)
    offsets = jax.vmap(one_row)(row_keys)[:, :K - 1].astype(jnp.int32)
    offsets = jnp.concatenate([jnp.zeros((NB, 1), jnp.int32), offsets], axis=1)
    density_level = jax.random.randint(jax.random.fold_in(key, 12), (NB // BR_DEV,), (K + 2) // 3, K + 1)
    jitter = jax.random.randint(jax.random.fold_in(key, 13), (NB,), 0, 2)
    counts = jnp.clip(jnp.repeat(density_level, BR_DEV) - jitter, 1, K)
    counts = counts.at[0].set(K)
    row_ids = jnp.arange(NB, dtype=jnp.int32)
    col_ids = (row_ids[:, None] + offsets) % NB
    slot_ids = jnp.arange(K, dtype=jnp.int32)
    return jnp.where(slot_ids[None, :] < counts[:, None], col_ids, -1).astype(jnp.int32)


def block_scale(stream_key, extent, pieces, low, top_value):
    def one(dim, blocks):
        steps = jax.random.uniform(jax.random.fold_in(jax.random.fold_in(stream_key, 6), dim), (blocks,), jnp.float32, low / len(pieces), top_value / len(pieces))
        return jnp.repeat(jnp.exp(steps), extent[dim] // blocks).reshape((-1,) + (1,) * (len(extent) - dim - 1))

    gain = one(*pieces[0])
    for cut in pieces[1:]:
        gain = gain * one(*cut)
    return gain


def bell_draw(stream_key, extent, deviation, most, cuts=(), kind=jnp.bfloat16):
    array = deviation * jax.random.normal(stream_key, extent, jnp.float32)
    if cuts:
        array = array * block_scale(stream_key, extent, cuts, -0.22, 0.18)
    return jnp.clip(array, -most, most).astype(kind)


def setup_inputs(seed: int = 0, part: int = 0) -> dict:
    key_list = jax.random.split(jax.random.key(seed), 3)
    part_splits = jax.random.split(jax.random.fold_in(key_list[2], part), 3)
    return {
        "matrix": bell_draw(part_splits[0], (NB, K, BS, BS), (2.0 / (3 * BS) ** 0.5), 1.5, ((0, 8), (1, 2))),
        "columns": draw_columns(jax.random.fold_in(key_list[2], 71), part),
    }


def restricted_product(left_blocks, right_blocks, columns):
    def one_row(inputs):
        left_row, col_row = inputs
        source = jnp.where(col_row >= 0, col_row, 0).astype(jnp.int32)
        right_rows = right_blocks[source].astype(jnp.float32)
        source_cols = columns[source]
        matches = (source_cols[:, None, :] == col_row[None, :, None]) & (col_row[:, None, None] >= 0) & (col_row[None, :, None] >= 0)
        picked = jnp.einsum('tsu,tuab->tsab', matches.astype(jnp.float32), right_rows)
        return jnp.einsum('tab,tsbc->sac', left_row.astype(jnp.float32), picked)
    return lax.map(one_row, (left_blocks, columns))


def reference(matrix, columns):
    valid_mask = (columns >= 0)[:, :, None, None]
    square = restricted_product(matrix, matrix, columns)
    square = jnp.where(valid_mask, square, jnp.float32(0.0)).astype(jnp.bfloat16)
    cube_sum = restricted_product(square, matrix, columns)
    result = 3.0 * square.astype(jnp.float32) - 2.0 * cube_sum
    return jnp.where(valid_mask, result, jnp.float32(0.0)).astype(jnp.bfloat16)
```

```python
import functools

import jax
import jax.numpy as jnp
from jax import lax
from jax.experimental import pallas as pl
from jax.experimental.pallas import tpu as pltpu
from jax.sharding import PartitionSpec as P

REACH = 4
ABSENT = 64


def purify_kernel(
    reach, flip_ref, table_ref, keep_ref, own_ref, other_ref, near_ref, cross_ref,
    stay_ref, leave_ref, own, other, near, cross, panel, square, result, sems
):
    rows, half, size = own.shape[0], own.shape[1], own.shape[2]
    width = rows + reach
    copies = []
    for n, (src, dst) in enumerate(
        [(own_ref, own), (other_ref, other), (near_ref, near), (cross_ref, cross)]
    ):
        copy = pltpu.make_async_copy(src, dst, sems.at[n])
        copy.start()
        copies.append(copy)
    panel[...] = jnp.zeros_like(panel)
    result[:, width * size :] = jnp.zeros((reach * size, size), result.dtype)
    flip = flip_ref[0]
    for copy in copies:
        copy.wait()

    for q in range(width):
        if q < reach:
            first, second = near, cross
            index = jnp.where(flip == 0, q, reach - 1 - q)
        else:
            first, second = own, other
            index = jnp.where(flip == 0, q - reach, width - 1 - q)
        for s in range(2 * half):
            place = pl.multiple_of(table_ref[q, s] * size, size)
            source = first if s < half else second
            panel[q * size : (q + 1) * size, pl.ds(place, size)] = source[index, s % half]

    def band_product(left, p):
        low = max(0, 2 * p - reach) * size
        high = min(width, 2 * p + 2 + reach) * size
        return jnp.dot(
            left[:, low:high],
            panel[low:high, 2 * p * size : (2 * p + 2) * size],
            preferred_element_type=jnp.float32,
        )

    left = panel.at[reach * size : 2 * reach * size]
    for p in range(width // 2):
        value = band_product(left, p)
        for i in range(reach):
            for k in (2 * p, 2 * p + 1):
                at = (slice(i * size, (i + 1) * size), slice(k * size, (k + 1) * size))
                if abs(i + reach - k) <= reach:
                    block = value[i * size : (i + 1) * size, (k - 2 * p) * size : (k - 2 * p + 1) * size]
                    square[at] = jnp.where(keep_ref[i, k] > 0, block, 0.0).astype(square.dtype)
                else:
                    square[at] = jnp.zeros((size, size), square.dtype)
    for p in range(width // 2):
        value = band_product(square, p)
        cols = slice(2 * p * size, (2 * p + 2) * size)
        result[:, cols] = (3.0 * square[:, cols].astype(jnp.float32) - 2.0 * value).astype(result.dtype)
    for i in range(reach):
        index = jnp.where(flip == 0, i, reach - 1 - i)
        for s in range(2 * half):
            place = pl.multiple_of(table_ref[i + reach, s] * size, size)
            target = stay_ref if s < half else leave_ref
            target[index, s % half] = result[i * size : (i + 1) * size, pl.ds(place, size)]


def purify(flip, table, keep, own, other, near, cross):
    rows, half, size = own.shape[:3]
    reach = near.shape[0]
    width = rows + reach
    smem = pl.BlockSpec(memory_space=pltpu.SMEM)
    anywhere = pl.BlockSpec(memory_space=pl.ANY)
    vmem = pl.BlockSpec(memory_space=pltpu.VMEM)
    out = jax.ShapeDtypeStruct((reach, half, size, size), own.dtype)
    return pl.pallas_call(
        functools.partial(purify_kernel, reach),
        out_shape=(out, out),
        in_specs=[smem] * 3 + [anywhere] * 4,
        out_specs=(vmem, vmem),
        scratch_shapes=[
            pltpu.VMEM(own.shape, own.dtype),
            pltpu.VMEM(own.shape, own.dtype),
            pltpu.VMEM(near.shape, own.dtype),
            pltpu.VMEM(near.shape, own.dtype),
            pltpu.VMEM((width * size, (width + 1) * size), own.dtype),
            pltpu.VMEM((reach * size, width * size), own.dtype),
            pltpu.VMEM((reach * size, (width + 1) * size), own.dtype),
            pltpu.SemaphoreType.DMA((4,)),
        ],
        compiler_params=pltpu.CompilerParams(vmem_limit_bytes=40 * 1024 * 1024),
        name="purify",
    )(flip, table, keep, own, other, near, cross)


def local(matrix, columns):
    local_rows, own_slots = matrix.shape[:2]
    reach = REACH
    cols = lax.axis_size("col")
    ring = lax.axis_size("row")
    total_rows = local_rows * ring
    row_start = lax.axis_index("row") * local_rows
    c = lax.axis_index("col")
    straight = c == 0
    width = local_rows + reach
    same = [(r * cols, (r + 1) % ring * cols) for r in range(ring)] + [
        (r * cols + 1, (r - 1) % ring * cols + 1) for r in range(ring)
    ]
    swap = [(r * cols + 1, (r + 1) % ring * cols) for r in range(ring)] + [
        (r * cols, (r - 1) % ring * cols + 1) for r in range(ring)
    ]
    axes = ("row", "col")
    start = jnp.where(straight, local_rows - reach, 0)
    other = lax.ppermute(matrix, "col", [(i, (i + 1) % cols) for i in range(cols)])
    near = lax.ppermute(lax.dynamic_slice_in_dim(matrix, start, reach, 0), axes, same)
    cross = lax.ppermute(
        lax.dynamic_slice_in_dim(matrix, local_rows - reach - start, reach, 0), axes, swap
    )
    row_ids = row_start + jnp.arange(local_rows, dtype=jnp.int32)[:, None]
    shift = (columns - row_ids + reach) % total_rows - reach
    shift = jnp.where(straight, shift, -shift)
    shift = jnp.where(columns >= 0, shift, ABSENT)
    halo_shift = lax.ppermute(lax.dynamic_slice_in_dim(shift, start, reach, 0), axes, same)
    both = jnp.concatenate(
        [jnp.where(straight, halo_shift, halo_shift[::-1]), jnp.where(straight, shift, shift[::-1])], axis=0
    )
    both = jnp.where(straight, both, jnp.roll(both, own_slots, axis=1))
    table = both + jnp.arange(width, dtype=jnp.int32)[:, None]
    table = jnp.where((table >= 0) & (table < width), table, width)
    keep = jnp.any(
        table[reach : 2 * reach, :, None] == jnp.arange(width, dtype=jnp.int32), axis=1
    ).astype(jnp.int32)
    flip = c.astype(jnp.int32).reshape(1)
    stay, leave = purify(flip, table, keep, matrix, other, near, cross)
    arrived = lax.ppermute(leave, "col", [(i, (i + 1) % cols) for i in range(cols)])
    return jnp.where(
        straight, jnp.concatenate([stay, arrived], axis=0), jnp.concatenate([arrived, stay], axis=0)
    )


def solution(mesh):
    placed = (P(("geom", "row"), "col", None, None), P("row", None))
    return jax.shard_map(
        local,
        mesh=mesh,
        in_specs=placed,
        out_specs=P(("geom", "row"), "col", None, None),
        check_vma=False,
    )
```

```python
import functools

import jax
import jax.numpy as jnp
from jax import lax
from jax.experimental import pallas as pl
from jax.experimental.pallas import tpu as pltpu
from jax.sharding import PartitionSpec as P

REACH = 4
ABSENT = 64
MIB = 1024 * 1024

SMEM = pl.BlockSpec(memory_space=pltpu.SMEM)
VMEM = pl.BlockSpec(memory_space=pltpu.VMEM)


def blocks(first, last, size):
    return slice(first * size, last * size)


def place_blocks(panel, base, q, index, table_ref, row, first, second):
    half, size = first.shape[1], first.shape[2]
    for s in range(2 * half):
        place = pl.multiple_of(table_ref[row, s] * size, size)
        source = first if s < half else second
        panel[blocks(q - base, q - base + 1, size), pl.ds(place, size)] = source[index, s % half]


def pack_kernel(far, reach, flip_ref, table_ref, own_ref, other_ref, out_ref):
    rows, half = own_ref.shape[:2]
    out_ref[...] = jnp.zeros_like(out_ref)
    for f in range(far):
        index = jnp.where(flip_ref[0] == 0, reach + f, rows - 1 - reach - f)
        for s in range(2 * half):
            place = table_ref[f, s]
            source = own_ref if s < half else other_ref

            @pl.when(place < out_ref.shape[0])
            def _(place=place, source=source, index=index, s=s):
                out_ref[place] = source[index, s % half]


def near_kernel(
    reach, far, flip_ref, table_ref, keep_ref, own_ref, other_ref, near_ref, cross_ref,
    stay_ref, leave_ref, part_ref, high_ref, cube_ref, lower_ref, panel, square, result
):
    rows, half, size = own_ref.shape[0], own_ref.shape[1], own_ref.shape[2]
    width = rows + reach
    low_cols = reach + far
    far_cols = 2 * reach + far
    near = reach - far
    flip = flip_ref[0]
    panel[...] = jnp.zeros_like(panel)
    result[:, blocks(width, width + 1, size)] = jnp.zeros((near * size, size), result.dtype)
    for q in range(far, width):
        if q < reach:
            index = jnp.where(flip == 0, q - far, reach - 1 - q)
            place_blocks(panel, far, q, index, table_ref, q, near_ref, cross_ref)
        else:
            index = jnp.where(flip == 0, q - reach, width - 1 - q)
            place_blocks(panel, far, q, index, table_ref, q, own_ref, other_ref)

    def band_product(left, p):
        low = max(far, 2 * p - reach)
        high = min(width, 2 * p + 2 + reach)
        return jnp.dot(
            left[:, blocks(low, high, size)],
            panel[blocks(low - far, high - far, size), blocks(2 * p, 2 * p + 2, size)],
            preferred_element_type=jnp.float32,
        )

    left = panel.at[blocks(reach - far, 2 * reach - far, size)]
    for p in range(width // 2):
        value = band_product(left, p)
        for i in range(reach):
            for k in (2 * p, 2 * p + 1):
                block = value[blocks(i, i + 1, size), blocks(k - 2 * p, k - 2 * p + 1, size)]
                at = (blocks(i, i + 1, size), blocks(k, k + 1, size))
                if i < far and k < low_cols:
                    part_ref[at] = block
                    square[at] = jnp.zeros((size, size), square.dtype)
                elif abs(i + reach - k) <= reach:
                    square[at] = jnp.where(keep_ref[i, k] > 0, block, 0.0).astype(square.dtype)
                else:
                    square[at] = jnp.zeros((size, size), square.dtype)
    for p in range(width // 2):
        value = band_product(square, p)
        cols = blocks(2 * p, 2 * p + 2, size)
        if 2 * p < far_cols:
            cube_ref[:, cols] = value[: far * size]
        result[:, cols] = (
            3.0 * square[far * size :, cols].astype(jnp.float32) - 2.0 * value[far * size :]
        ).astype(result.dtype)
    high_ref[...] = square[: far * size, blocks(low_cols, far_cols, size)]
    lower_ref[...] = panel[blocks(0, low_cols - far, size), blocks(0, far_cols, size)]
    for i in range(near):
        index = jnp.where(flip == 0, i, near - 1 - i)
        for s in range(2 * half):
            place = pl.multiple_of(table_ref[i + reach + far, s] * size, size)
            target = stay_ref if s < half else leave_ref
            target[index, s % half] = result[blocks(i, i + 1, size), pl.ds(place, size)]


def far_kernel(
    reach, far, flip_ref, table_ref, keep_ref, far_ref, part_ref, high_ref, cube_ref, lower_ref,
    stay_ref, leave_ref, panel, square, result
):
    half, size = stay_ref.shape[1], stay_ref.shape[2]
    low_cols = reach + far
    far_cols = 2 * reach + far
    at = 0
    for f in range(far):
        for k in range(low_cols):
            here = (blocks(f, f + 1, size), blocks(k, k + 1, size))
            if k <= f + reach:
                panel[here] = far_ref[at]
                at += 1
            else:
                panel[here] = jnp.zeros((size, size), panel.dtype)
    result[:, blocks(far_cols, far_cols + 1, size)] = jnp.zeros((far * size, size), result.dtype)
    left = lower_ref[blocks(reach - far, reach, size), blocks(0, far, size)]
    for p in range(low_cols // 2):
        cols = blocks(2 * p, 2 * p + 2, size)
        value = part_ref[:, cols] + jnp.dot(left, panel[:, cols], preferred_element_type=jnp.float32)
        for i in range(far):
            for k in (2 * p, 2 * p + 1):
                block = value[blocks(i, i + 1, size), blocks(k - 2 * p, k - 2 * p + 1, size)]
                here = (blocks(i, i + 1, size), blocks(k, k + 1, size))
                if abs(i + reach - k) <= reach:
                    square[here] = jnp.where(keep_ref[i, k] > 0, block, 0.0).astype(square.dtype)
                else:
                    square[here] = jnp.zeros((size, size), square.dtype)
    for p in range(far_cols // 2):
        cols = blocks(2 * p, 2 * p + 2, size)
        value = cube_ref[:, cols] + jnp.dot(
            square[:, blocks(far, low_cols, size)], lower_ref[:, cols], preferred_element_type=jnp.float32
        )
        if 2 * p < low_cols:
            value = value + jnp.dot(
                square[:, blocks(0, far, size)], panel[:, cols], preferred_element_type=jnp.float32
            )
            kept = square[:, cols]
        else:
            kept = high_ref[:, blocks(2 * p - low_cols, 2 * p + 2 - low_cols, size)]
        result[:, cols] = (3.0 * kept.astype(jnp.float32) - 2.0 * value).astype(result.dtype)
    for i in range(far):
        index = jnp.where(flip_ref[0] == 0, i, far - 1 - i)
        for s in range(2 * half):
            place = pl.multiple_of(table_ref[i, s] * size, size)
            target = stay_ref if s < half else leave_ref
            target[index, s % half] = result[blocks(i, i + 1, size), pl.ds(place, size)]


def local(matrix, columns):
    local_rows, own_slots, size = matrix.shape[:3]
    dtype = matrix.dtype
    reach = REACH
    far = reach // 2
    near = reach - far
    cols = lax.axis_size("col")
    ring = lax.axis_size("row")
    total_rows = local_rows * ring
    row_start = lax.axis_index("row") * local_rows
    c = lax.axis_index("col")
    straight = c == 0
    flip = c.astype(jnp.int32).reshape(1)
    width = local_rows + reach
    same = [(r * cols, (r + 1) % ring * cols) for r in range(ring)] + [
        (r * cols + 1, (r - 1) % ring * cols + 1) for r in range(ring)
    ]
    swap = [(r * cols + 1, (r + 1) % ring * cols) for r in range(ring)] + [
        (r * cols, (r - 1) % ring * cols + 1) for r in range(ring)
    ]
    beside = [(i, (i + 1) % cols) for i in range(cols)]
    axes = ("row", "col")
    start = jnp.where(straight, local_rows - near, 0)
    other = lax.ppermute(matrix, "col", beside)
    near_rows = lax.ppermute(lax.dynamic_slice_in_dim(matrix, start, near, 0), axes, same)
    cross_rows = lax.ppermute(
        lax.dynamic_slice_in_dim(matrix, local_rows - near - start, near, 0), axes, swap
    )
    row_ids = row_start + jnp.arange(local_rows, dtype=jnp.int32)[:, None]
    shift = (columns - row_ids + reach) % total_rows - reach
    shift = jnp.where(straight, shift, -shift)
    shift = jnp.where(columns >= 0, shift, ABSENT)

    def arrange(rows):
        rows = jnp.where(straight, rows, rows[::-1])
        return jnp.where(straight, rows, jnp.roll(rows, own_slots, axis=1))

    own_shift = arrange(shift)
    count = [reach + 1 + f for f in range(far)]
    first = jnp.array([sum(count[:f]) for f in range(far)], jnp.int32)[:, None]
    f_ids = jnp.arange(far, dtype=jnp.int32)[:, None]
    sent = own_shift[reach : reach + far] + f_ids
    pack_table = jnp.where((sent >= 0) & (sent <= reach + f_ids), first + sent, ABSENT)
    packed = pl.pallas_call(
        functools.partial(pack_kernel, far, reach),
        out_shape=jax.ShapeDtypeStruct((sum(count), size, size), dtype),
        in_specs=[SMEM, SMEM, VMEM, VMEM],
        out_specs=VMEM,
        name="pack",
    )(flip, pack_table, matrix, other)
    far_blocks = lax.ppermute(packed, axes, same)

    halo_shift = arrange(lax.ppermute(lax.dynamic_slice_in_dim(shift, start, near, 0), axes, same))
    table = jnp.concatenate([jnp.full((far, 2 * own_slots), ABSENT, jnp.int32), halo_shift, own_shift], axis=0)
    table = table + jnp.arange(width, dtype=jnp.int32)[:, None]
    table = jnp.where((table >= 0) & (table < width), table, width)
    own_table = table[reach : 2 * reach]
    keep = jnp.any(own_table[:, :, None] == jnp.arange(width, dtype=jnp.int32), axis=1).astype(jnp.int32)

    low_cols = reach + far
    far_cols = 2 * reach + far
    rows_out = jax.ShapeDtypeStruct((near, own_slots, size, size), dtype)
    stay_near, leave_near, part, high, cube, lower = pl.pallas_call(
        functools.partial(near_kernel, reach, far),
        out_shape=(
            rows_out,
            rows_out,
            jax.ShapeDtypeStruct((far * size, low_cols * size), jnp.float32),
            jax.ShapeDtypeStruct((far * size, (far_cols - low_cols) * size), dtype),
            jax.ShapeDtypeStruct((far * size, far_cols * size), jnp.float32),
            jax.ShapeDtypeStruct(((low_cols - far) * size, far_cols * size), dtype),
        ),
        in_specs=[SMEM] * 3 + [VMEM] * 4,
        out_specs=(VMEM,) * 6,
        scratch_shapes=[
            pltpu.VMEM(((width - far) * size, (width + 1) * size), dtype),
            pltpu.VMEM((reach * size, width * size), dtype),
            pltpu.VMEM((near * size, (width + 1) * size), dtype),
        ],
        compiler_params=pltpu.CompilerParams(vmem_limit_bytes=24 * MIB),
        name="near",
    )(flip, table, keep, matrix, other, near_rows, cross_rows)
    arrived_near = lax.ppermute(leave_near, "col", beside)

    far_table = own_table[:far]
    far_table = jnp.where(far_table < width, far_table, far_cols)
    far_out = jax.ShapeDtypeStruct((far, own_slots, size, size), dtype)
    stay_far, leave_far = pl.pallas_call(
        functools.partial(far_kernel, reach, far),
        out_shape=(far_out, far_out),
        in_specs=[SMEM] * 3 + [VMEM] * 5,
        out_specs=(VMEM,) * 2,
        scratch_shapes=[
            pltpu.VMEM((far * size, low_cols * size), dtype),
            pltpu.VMEM((far * size, low_cols * size), dtype),
            pltpu.VMEM((far * size, (far_cols + 1) * size), dtype),
        ],
        compiler_params=pltpu.CompilerParams(vmem_limit_bytes=24 * MIB),
        name="far",
    )(flip, far_table, keep, far_blocks, part, high, cube, lower)
    arrived_far = lax.ppermute(leave_far, "col", beside)
    return jnp.where(
        straight,
        jnp.concatenate([stay_far, stay_near, arrived_near, arrived_far], axis=0),
        jnp.concatenate([arrived_far, arrived_near, stay_near, stay_far], axis=0),
    )


def solution(mesh):
    placed = (P(("geom", "row"), "col", None, None), P("row", None))
    return jax.shard_map(
        local,
        mesh=mesh,
        in_specs=placed,
        out_specs=P(("geom", "row"), "col", None, None),
        check_vma=False,
    )
```

```python
import functools

import jax
import jax.numpy as jnp
from jax import lax
from jax.experimental import pallas as pl
from jax.experimental.pallas import tpu as pltpu
from jax.sharding import PartitionSpec as P

REACH = 4
MIB = 1024 * 1024
ABSENT = 64
TILE = 16

HEAVY = pl.CostEstimate(flops=20_000_000_000, bytes_accessed=0, transcendentals=0)
LIGHT = pl.CostEstimate(flops=0, bytes_accessed=0, transcendentals=0)

SMEM = pl.BlockSpec(memory_space=pltpu.SMEM)
VMEM = pl.BlockSpec(memory_space=pltpu.VMEM)
ANY = pl.BlockSpec(memory_space=pl.ANY)
HBM = pl.BlockSpec(memory_space=pltpu.HBM)


def limit(mib):
    return pltpu.CompilerParams(vmem_limit_bytes=mib * MIB)


def blocks(first, last, size):
    return slice(first * size, last * size)


def own_place(columns_ref, q, s, limit):
    rows, slots = columns_ref.shape
    flip = lax.axis_index("col")
    row = jnp.where(flip == 0, q - REACH, rows + REACH - 1 - q)
    slot = lax.rem(s + flip * (slots // 2), slots)
    total = rows * lax.axis_size("row")
    column = columns_ref[row, slot]
    step = column - lax.axis_index("row") * rows - row
    step = jnp.where(step > REACH, step - total, step)
    step = jnp.where(step < -REACH, step + total, step)
    place = jnp.where(flip == 0, q + step, q - step)
    inside = (column >= 0) & (place >= 0) & (place < limit)
    return jnp.where(inside, place, limit)


def halo_place(steps_ref, rows, slots, q, s, limit):
    flip = lax.axis_index("col")
    row = jnp.where(flip == 0, rows - REACH + q, REACH - 1 - q)
    slot = lax.rem(s + flip * (slots // 2), slots)
    step = steps_ref[row, slot]
    place = jnp.where(flip == 0, q + step, q - step)
    inside = (step <= REACH) & (place >= 0) & (place < limit)
    return jnp.where(inside, place, limit)


def edge_kernel(near, columns_ref, matrix_ref, same_ref, swap_ref, copied_ref, steps, sems):
    rows, half, size = matrix_ref.shape[:3]
    start = jnp.where(lax.axis_index("col") == 0, rows - near, 0)
    copies = []
    for n in range(near):
        for s in range(half):
            at = blocks(n * half + s, n * half + s + 1, size)
            copies.append(pltpu.make_async_copy(matrix_ref.at[start + n, s], same_ref.at[at], sems.at[0]))
            copies.append(
                pltpu.make_async_copy(
                    matrix_ref.at[rows - near - start + n, s], swap_ref.at[at], sems.at[1]
                )
            )
    held = pltpu.make_async_copy(columns_ref, copied_ref, sems.at[2])
    held.start()
    for copy in copies:
        copy.start()
    held.wait()
    column = copied_ref[...]
    row = lax.broadcasted_iota(jnp.int32, column.shape, 0) + lax.axis_index("row") * rows
    total = rows * lax.axis_size("row")
    step = column - row
    step = jnp.where(step > REACH, step - total, step)
    step = jnp.where(step < -REACH, step + total, step)
    step = jnp.where(column >= 0, step, ABSENT)
    steps[...] = jnp.zeros_like(steps)
    steps[:rows, : column.shape[1]] = step.astype(jnp.float32)
    same_ref[near * half * size :, :] = steps[...].astype(same_ref.dtype)
    for copy in copies:
        copy.wait()


def base_kernel(far, columns_ref, own_ref, other_ref, panel_ref, first_ref):
    rows, half, size = own_ref.shape[0], own_ref.shape[1], own_ref.shape[2]
    reach = REACH
    width = rows + reach
    panel_ref[...] = jnp.zeros_like(panel_ref)
    for q in reversed(range(reach, width)):
        index = jnp.where(lax.axis_index("col") == 0, q - reach, width - 1 - q)
        for s in range(2 * half):
            place = pl.multiple_of(own_place(columns_ref, q, s, width + far) * size, size)
            source = own_ref if s < half else other_ref
            panel_ref[blocks(q - reach, q - reach + 1, size), pl.ds(place, size)] = source[index, s % half]
    for p in range(width // 2):
        low = max(reach, 2 * p - reach)
        high = min(width, 2 * p + 2 + reach)
        cols = blocks(2 * p, 2 * p + 2, size)
        first_ref[:, cols] = jnp.dot(
            panel_ref[blocks(0, reach, size), blocks(low, high, size)],
            panel_ref[blocks(low - reach, high - reach, size), cols],
            preferred_element_type=jnp.float32,
        )


def pack_kernel(far, panel_ref, after_ref, out_ref):
    size = out_ref.shape[1]
    at = 0
    for f in range(far):
        row = REACH + f
        for k in range(2 * REACH, 3 * REACH + 1 + f):
            out_ref[at] = panel_ref[blocks(row, row + 1, size), blocks(k, k + 1, size)]
            at += 1


def mark_kept(columns_ref, keep_ref, count):
    width = columns_ref.shape[0] + REACH
    for i in range(count):
        for k in range(width + 1):
            keep_ref[i, k] = 0
        for s in range(columns_ref.shape[1]):
            keep_ref[i, own_place(columns_ref, i + REACH, s, width)] = 1


def near_kernel(
    far, columns_ref, panel_ref, first_ref, near_ref, cross_ref,
    stay_ref, leave_ref, part_ref, high_ref, cube_ref, lower_ref,
    square, result, keep_ref, steps, halo_ref, sem
):
    reach = REACH
    half, size = stay_ref.shape[1], stay_ref.shape[2]
    steps[...] = near_ref[(reach - far) * half * size :, :].astype(jnp.float32).astype(jnp.int32)
    copy = pltpu.make_async_copy(steps, halo_ref, sem)
    copy.start()
    width = panel_ref.shape[0] // size + reach
    near = reach - far
    low_cols = reach + far
    far_cols = 2 * reach + far
    near_cols = 2 * reach
    flip = lax.axis_index("col")
    mark_kept(columns_ref, keep_ref, reach)
    lower_ref[...] = jnp.zeros_like(lower_ref)
    result[:, blocks(width, width + 1, size)] = jnp.zeros((near * size, size), result.dtype)
    copy.wait()
    for n in range(near):
        index = jnp.where(flip == 0, n, near - 1 - n)
        for s in range(2 * half):
            place = halo_place(halo_ref, *columns_ref.shape, n + far, s, near_cols)
            place = pl.multiple_of(place * size, size)
            source = near_ref if s < half else cross_ref
            at = pl.multiple_of((index * half + s % half) * size, size)
            lower_ref[blocks(n, n + 1, size), pl.ds(place, size)] = source[pl.ds(at, size)]
    left = panel_ref.at[blocks(0, reach, size), blocks(far, reach, size)]
    for p in range(width // 2):
        cols = blocks(2 * p, 2 * p + 2, size)
        value = first_ref[:, cols]
        if 2 * p < near_cols:
            value = value + jnp.dot(left[...], lower_ref[:, cols], preferred_element_type=jnp.float32)
        for i in range(reach):
            for k in (2 * p, 2 * p + 1):
                block = value[blocks(i, i + 1, size), blocks(k - 2 * p, k - 2 * p + 1, size)]
                at = (blocks(i, i + 1, size), blocks(k, k + 1, size))
                if i < far and k < low_cols:
                    part_ref[at] = block
                    square[at] = jnp.zeros((size, size), square.dtype)
                elif abs(i + reach - k) <= reach:
                    square[at] = jnp.where(keep_ref[i, k] > 0, block, 0.0).astype(square.dtype)
                else:
                    square[at] = jnp.zeros((size, size), square.dtype)
    for p in range(width // 2):
        cols = blocks(2 * p, 2 * p + 2, size)
        low = max(reach, 2 * p - reach)
        high = min(width, 2 * p + 2 + reach)
        value = jnp.dot(
            square[:, blocks(low, high, size)],
            panel_ref[blocks(low - reach, high - reach, size), cols],
            preferred_element_type=jnp.float32,
        )
        if 2 * p < near_cols:
            value = value + jnp.dot(
                square[:, blocks(far, reach, size)], lower_ref[:, cols], preferred_element_type=jnp.float32
            )
        if 2 * p < far_cols:
            cube_ref[:, cols] = value[: far * size]
        result[:, cols] = (
            3.0 * square[far * size :, cols].astype(jnp.float32) - 2.0 * value[far * size :]
        ).astype(result.dtype)
    high_ref[...] = square[: far * size, blocks(low_cols, far_cols, size)]
    for i in range(near):
        index = jnp.where(flip == 0, i, near - 1 - i)
        for s in range(2 * half):
            place = pl.multiple_of(own_place(columns_ref, i + reach + far, s, width) * size, size)
            target = stay_ref if s < half else leave_ref
            target[index, s % half] = result[blocks(i, i + 1, size), pl.ds(place, size)]


def far_kernel(
    columns_ref, far_ref, part_ref, high_ref, cube_ref, lower_ref, panel_ref, kept_near_ref, got_near_ref,
    stay_ref, leave_ref, out_ref, farthest, square, result, keep_ref, sems
):
    reach, far = REACH, stay_ref.shape[0]
    copies = placed(kept_near_ref, got_near_ref, out_ref, far, sems)
    half, size = stay_ref.shape[1], stay_ref.shape[2]
    low_cols = reach + far
    far_cols = 2 * reach + far
    near_cols = 2 * reach
    mark_kept(columns_ref, keep_ref, far)
    at = 0
    for f in range(far):
        for k in range(low_cols):
            here = (blocks(f, f + 1, size), blocks(k, k + 1, size))
            if k <= f + reach:
                farthest[here] = far_ref[at]
                at += 1
            else:
                farthest[here] = jnp.zeros((size, size), farthest.dtype)
    result[:, blocks(far_cols, far_cols + 1, size)] = jnp.zeros((far * size, size), result.dtype)
    left = panel_ref[blocks(0, far, size), blocks(0, far, size)]
    for p in range(low_cols // 2):
        cols = blocks(2 * p, 2 * p + 2, size)
        value = part_ref[:, cols] + jnp.dot(left, farthest[:, cols], preferred_element_type=jnp.float32)
        for i in range(far):
            for k in (2 * p, 2 * p + 1):
                block = value[blocks(i, i + 1, size), blocks(k - 2 * p, k - 2 * p + 1, size)]
                here = (blocks(i, i + 1, size), blocks(k, k + 1, size))
                if abs(i + reach - k) <= reach:
                    square[here] = jnp.where(keep_ref[i, k] > 0, block, 0.0).astype(square.dtype)
                else:
                    square[here] = jnp.zeros((size, size), square.dtype)
    for p in range(far_cols // 2):
        cols = blocks(2 * p, 2 * p + 2, size)
        value = cube_ref[:, cols] + jnp.dot(
            square[:, blocks(reach, low_cols, size)],
            panel_ref[blocks(0, far, size), cols],
            preferred_element_type=jnp.float32,
        )
        if 2 * p < near_cols:
            value = value + jnp.dot(
                square[:, blocks(far, reach, size)], lower_ref[:, cols], preferred_element_type=jnp.float32
            )
        if 2 * p < low_cols:
            value = value + jnp.dot(
                square[:, blocks(0, far, size)], farthest[:, cols], preferred_element_type=jnp.float32
            )
            kept = square[:, cols]
        else:
            kept = high_ref[:, blocks(2 * p - low_cols, 2 * p + 2 - low_cols, size)]
        result[:, cols] = (3.0 * kept.astype(jnp.float32) - 2.0 * value).astype(result.dtype)
    for i in range(far):
        index = jnp.where(lax.axis_index("col") == 0, i, far - 1 - i)
        for s in range(2 * half):
            place = pl.multiple_of(own_place(columns_ref, i + reach, s, far_cols) * size, size)
            target = stay_ref if s < half else leave_ref
            target[index, s % half] = result[blocks(i, i + 1, size), pl.ds(place, size)]
    for copy in copies:
        copy.wait()


def placed(kept_ref, got_ref, out_ref, inner, sems):
    rows, count = out_ref.shape[0], kept_ref.shape[0]
    straight = lax.axis_index("col") == 0
    low, high = inner, rows - inner - count
    copies = []
    for n in range(count):
        copies.append(
            pltpu.make_async_copy(
                kept_ref.at[n], out_ref.at[jnp.where(straight, low, high) + n], sems.at[0]
            )
        )
        copies.append(
            pltpu.make_async_copy(got_ref.at[n], out_ref.at[jnp.where(straight, high, low) + n], sems.at[1])
        )
    for copy in copies:
        copy.start()
    return copies


def finish_kernel(kept_ref, got_ref, before_ref, out_ref, sems):
    for copy in placed(kept_ref, got_ref, out_ref, 0, sems):
        copy.wait()


def local(matrix, columns):
    local_rows, own_slots, size = matrix.shape[:3]
    dtype = matrix.dtype
    reach = REACH
    far = reach // 2
    near = reach - far
    cols = lax.axis_size("col")
    ring = lax.axis_size("row")
    width = local_rows + reach
    low_cols = reach + far
    far_cols = 2 * reach + far
    near_cols = 2 * reach
    same = [(r * cols, (r + 1) % ring * cols) for r in range(ring)] + [
        (r * cols + 1, (r - 1) % ring * cols + 1) for r in range(ring)
    ]
    swap = [(r * cols + 1, (r + 1) % ring * cols) for r in range(ring)] + [
        (r * cols, (r - 1) % ring * cols + 1) for r in range(ring)
    ]
    beside = [(i, (i + 1) % cols) for i in range(cols)]
    axes = ("row", "col")
    edge_rows = near * own_slots * size
    to_same, to_swap, held = pl.pallas_call(
        functools.partial(edge_kernel, near),
        out_shape=(
            jax.ShapeDtypeStruct((edge_rows + TILE, size), dtype),
            jax.ShapeDtypeStruct((edge_rows, size), dtype),
            jax.ShapeDtypeStruct(columns.shape, columns.dtype),
        ),
        in_specs=[HBM, HBM],
        out_specs=(VMEM, VMEM, VMEM),
        scratch_shapes=[pltpu.VMEM((TILE, size), jnp.float32), pltpu.SemaphoreType.DMA((3,))],
        compiler_params=limit(1),
        cost_estimate=LIGHT,
        name="edge",
    )(
        pltpu.with_memory_space_constraint(columns, pltpu.HBM),
        pltpu.with_memory_space_constraint(matrix, pltpu.HBM),
    )
    near_rows = lax.ppermute(to_same, axes, same)
    cross_rows = lax.ppermute(to_swap, axes, swap)
    other = lax.ppermute(matrix, "col", beside)

    panel, first_part = pl.pallas_call(
        functools.partial(base_kernel, far),
        out_shape=(
            jax.ShapeDtypeStruct((local_rows * size, (width + far + 1) * size), dtype),
            jax.ShapeDtypeStruct((reach * size, width * size), jnp.float32),
        ),
        in_specs=[SMEM, VMEM, VMEM],
        out_specs=(VMEM, VMEM),
        compiler_params=limit(12),
        cost_estimate=LIGHT,
        name="base",
    )(held, matrix, other)
    packed = pl.pallas_call(
        functools.partial(pack_kernel, far),
        out_shape=jax.ShapeDtypeStruct((sum(reach + 1 + f for f in range(far)), size, size), dtype),
        in_specs=[VMEM, ANY],
        out_specs=VMEM,
        compiler_params=limit(1),
        cost_estimate=LIGHT,
        name="pack",
    )(panel, cross_rows)
    far_blocks = lax.ppermute(packed, axes, same)

    rows_out = jax.ShapeDtypeStruct((near, own_slots, size, size), dtype)
    stay_near, leave_near, part, high, cube, lower = pl.pallas_call(
        functools.partial(near_kernel, far),
        out_shape=(
            rows_out,
            rows_out,
            jax.ShapeDtypeStruct((far * size, low_cols * size), jnp.float32),
            jax.ShapeDtypeStruct((far * size, (far_cols - low_cols) * size), dtype),
            jax.ShapeDtypeStruct((far * size, far_cols * size), jnp.float32),
            jax.ShapeDtypeStruct((near * size, (near_cols + 1) * size), dtype),
        ),
        in_specs=[SMEM] + [VMEM] * 4,
        out_specs=(VMEM,) * 6,
        scratch_shapes=[
            pltpu.VMEM((reach * size, width * size), dtype),
            pltpu.VMEM((near * size, (width + 1) * size), dtype),
            pltpu.SMEM((reach, width + 1), jnp.int32),
            pltpu.VMEM((TILE, size), jnp.int32),
            pltpu.SMEM((TILE, size), jnp.int32),
            pltpu.SemaphoreType.DMA,
        ],
        compiler_params=limit(16),
        cost_estimate=HEAVY,
        name="near",
    )(held, panel, first_part, near_rows, cross_rows)
    arrived_near = lax.ppermute(leave_near, "col", beside)

    far_out = jax.ShapeDtypeStruct((far, own_slots, size, size), dtype)
    stay_far, leave_far, out = pl.pallas_call(
        far_kernel,
        out_shape=(far_out, far_out, jax.ShapeDtypeStruct(matrix.shape, dtype)),
        in_specs=[SMEM] + [VMEM] * 8,
        out_specs=(VMEM, VMEM, HBM),
        scratch_shapes=[
            pltpu.VMEM((far * size, low_cols * size), dtype),
            pltpu.VMEM((far * size, low_cols * size), dtype),
            pltpu.VMEM((far * size, (far_cols + 1) * size), dtype),
            pltpu.SMEM((far, width + 1), jnp.int32),
            pltpu.SemaphoreType.DMA((2,)),
        ],
        compiler_params=limit(16),
        cost_estimate=LIGHT,
        name="far",
    )(held, far_blocks, part, high, cube, lower, panel, stay_near, arrived_near)
    arrived_far = lax.ppermute(leave_far, "col", beside)
    return pl.pallas_call(
        finish_kernel,
        out_shape=jax.ShapeDtypeStruct(matrix.shape, dtype),
        in_specs=[VMEM, VMEM, HBM],
        out_specs=HBM,
        input_output_aliases={2: 0},
        scratch_shapes=[pltpu.SemaphoreType.DMA((2,))],
        compiler_params=limit(1),
        cost_estimate=LIGHT,
        name="finish",
    )(stay_far, arrived_far, out)


def solution(mesh):
    placed = (P(("geom", "row"), "col", None, None), P("row", None))
    return jax.shard_map(
        local,
        mesh=mesh,
        in_specs=placed,
        out_specs=P(("geom", "row"), "col", None, None),
        check_vma=False,
    )
```

```python
import functools

import jax
import jax.numpy as jnp
from jax import lax
from jax.experimental import pallas as pl
from jax.experimental.pallas import tpu as pltpu
from jax.sharding import PartitionSpec as P

REACH = 4
MIB = 1024 * 1024
ABSENT = 64
TILE = 16

HEAVY = pl.CostEstimate(flops=20_000_000_000, bytes_accessed=0, transcendentals=0)
LIGHT = pl.CostEstimate(flops=0, bytes_accessed=0, transcendentals=0)

SMEM = pl.BlockSpec(memory_space=pltpu.SMEM)
VMEM = pl.BlockSpec(memory_space=pltpu.VMEM)
ANY = pl.BlockSpec(memory_space=pl.ANY)
HBM = pl.BlockSpec(memory_space=pltpu.HBM)


def limit(mib):
    return pltpu.CompilerParams(vmem_limit_bytes=mib * MIB)


def blocks(first, last, size):
    return slice(first * size, last * size)


def own_place(columns_ref, q, s, limit):
    rows, slots = columns_ref.shape
    flip = lax.axis_index("col")
    row = jnp.where(flip == 0, q - REACH, rows + REACH - 1 - q)
    slot = lax.rem(s + flip * (slots // 2), slots)
    total = rows * lax.axis_size("row")
    column = columns_ref[row, slot]
    step = column - lax.axis_index("row") * rows - row
    step = jnp.where(step > REACH, step - total, step)
    step = jnp.where(step < -REACH, step + total, step)
    place = jnp.where(flip == 0, q + step, q - step)
    inside = (column >= 0) & (place >= 0) & (place < limit)
    return jnp.where(inside, place, limit)


def halo_place(steps_ref, rows, slots, q, s, limit):
    flip = lax.axis_index("col")
    row = jnp.where(flip == 0, rows - REACH + q, REACH - 1 - q)
    slot = lax.rem(s + flip * (slots // 2), slots)
    step = steps_ref[row, slot]
    place = jnp.where(flip == 0, q + step, q - step)
    inside = (step <= REACH) & (place >= 0) & (place < limit)
    return jnp.where(inside, place, limit)


def edge_kernel(near, columns_ref, matrix_ref, *refs):
    rows, half, size = matrix_ref.shape[:3]
    same_refs, swap_refs = refs[:near], refs[near : 2 * near]
    copied_ref, steps, sems = refs[2 * near :]
    straight = lax.axis_index("col") == 0
    copies = []
    for n in range(near):
        up, down = rows - 1 - n, n
        for s in range(half):
            at = blocks(s, s + 1, size)
            source = matrix_ref.at[jnp.where(straight, up, down), s]
            copies.append(pltpu.make_async_copy(source, same_refs[n].at[at], sems.at[0]))
            source = matrix_ref.at[jnp.where(straight, down, up), s]
            copies.append(pltpu.make_async_copy(source, swap_refs[n].at[at], sems.at[1]))
    held = pltpu.make_async_copy(columns_ref, copied_ref, sems.at[2])
    held.start()
    for copy in copies:
        copy.start()
    held.wait()
    column = copied_ref[...]
    row = lax.broadcasted_iota(jnp.int32, column.shape, 0) + lax.axis_index("row") * rows
    total = rows * lax.axis_size("row")
    step = column - row
    step = jnp.where(step > REACH, step - total, step)
    step = jnp.where(step < -REACH, step + total, step)
    step = jnp.where(column >= 0, step, ABSENT)
    steps[...] = jnp.zeros_like(steps)
    steps[:rows, : column.shape[1]] = step.astype(jnp.float32)
    same_refs[0][half * size :, :] = steps[...].astype(same_refs[0].dtype)
    for copy in copies:
        copy.wait()


def base_kernel(far, columns_ref, own_ref, other_ref, panel_ref, first_ref):
    rows, half, size = own_ref.shape[0], own_ref.shape[1], own_ref.shape[2]
    reach = REACH
    width = rows + reach
    panel_ref[...] = jnp.zeros_like(panel_ref)
    for q in reversed(range(reach, width)):
        index = jnp.where(lax.axis_index("col") == 0, q - reach, width - 1 - q)
        for s in range(2 * half):
            place = pl.multiple_of(own_place(columns_ref, q, s, width) * size, size)
            source = own_ref if s < half else other_ref
            panel_ref[blocks(q - reach, q - reach + 1, size), pl.ds(place, size)] = source[index, s % half]
    for p in range(width // 2):
        low = max(reach, 2 * p - reach)
        high = min(width, 2 * p + 2 + reach)
        cols = blocks(2 * p, 2 * p + 2, size)
        first_ref[:, cols] = jnp.dot(
            panel_ref[blocks(0, reach, size), blocks(low, high, size)],
            panel_ref[blocks(low - reach, high - reach, size), cols],
            preferred_element_type=jnp.float32,
        )


def pack_kernel(far, panel_ref, after_ref, out_ref):
    size = out_ref.shape[1]
    at = 0
    for f in range(far):
        row = REACH - 1 - f
        for k in range(2 * REACH - 1, REACH - 2 - f, -1):
            out_ref[at] = panel_ref[blocks(row, row + 1, size), blocks(k, k + 1, size)]
            at += 1


def mark_kept(columns_ref, keep_ref, count):
    width = columns_ref.shape[0] + REACH
    for i in range(count):
        for k in range(width + 1):
            keep_ref[i, k] = 0
        for s in range(columns_ref.shape[1]):
            keep_ref[i, own_place(columns_ref, i + REACH, s, width)] = 1


def near_kernel(
    far, held_ref, panel_ref, first_ref, *refs
):
    reach = REACH
    same_refs, swap_refs = refs[: reach - far], refs[reach - far : 2 * (reach - far)]
    (
        stay_ref, leave_ref, mask_ref, part_ref, high_ref, cube_ref, lower_ref,
        square, result, keep_ref, columns_ref, steps, halo_ref, sems,
    ) = refs[2 * (reach - far) :]
    half, size = stay_ref.shape[1], stay_ref.shape[2]
    steps[...] = same_refs[0][half * size :, :].astype(jnp.float32).astype(jnp.int32)
    copies = [
        pltpu.make_async_copy(held_ref, columns_ref, sems.at[0]),
        pltpu.make_async_copy(steps, halo_ref, sems.at[1]),
    ]
    for copy in copies:
        copy.start()
    width = panel_ref.shape[0] // size + reach
    near = reach - far
    low_cols = reach + far
    far_cols = 2 * reach + far
    near_cols = 2 * reach
    flip = lax.axis_index("col")
    lower_ref[...] = jnp.zeros_like(lower_ref)
    result[:, blocks(width, width + 1, size)] = jnp.zeros((near * size, size), result.dtype)
    for copy in copies:
        copy.wait()
    mark_kept(columns_ref, keep_ref, reach)
    for n in range(near):
        sources = same_refs[near - 1 - n], swap_refs[near - 1 - n]
        for s in range(2 * half):
            place = halo_place(halo_ref, *columns_ref.shape, n + far, s, near_cols)
            place = pl.multiple_of(place * size, size)
            at = blocks(s % half, s % half + 1, size)
            lower_ref[blocks(n, n + 1, size), pl.ds(place, size)] = sources[s // half][at, :]
    left = panel_ref.at[blocks(0, reach, size), blocks(far, reach, size)]
    for p in range(width // 2):
        cols = blocks(2 * p, 2 * p + 2, size)
        value = first_ref[:, cols]
        if 2 * p < near_cols:
            value = value + jnp.dot(left[...], lower_ref[:, cols], preferred_element_type=jnp.float32)
        for i in range(reach):
            for k in (2 * p, 2 * p + 1):
                block = value[blocks(i, i + 1, size), blocks(k - 2 * p, k - 2 * p + 1, size)]
                at = (blocks(i, i + 1, size), blocks(k, k + 1, size))
                if i < far and k < low_cols:
                    part_ref[at] = block
                    kept = jnp.full((1, size), keep_ref[i, k], jnp.float32)
                    mask_ref[i * low_cols + k : i * low_cols + k + 1, :] = kept
                    square[at] = jnp.zeros((size, size), square.dtype)
                elif abs(i + reach - k) <= reach:
                    square[at] = jnp.where(keep_ref[i, k] > 0, block, 0.0).astype(square.dtype)
                else:
                    square[at] = jnp.zeros((size, size), square.dtype)
    for p in range(width // 2):
        cols = blocks(2 * p, 2 * p + 2, size)
        low = max(reach, 2 * p - reach)
        high = min(width, 2 * p + 2 + reach)
        rest = slice(far * size, reach * size)
        value = jnp.dot(
            square[rest, blocks(low, high, size)],
            panel_ref[blocks(low - reach, high - reach, size), cols],
            preferred_element_type=jnp.float32,
        )
        if 2 * p < near_cols:
            value = value + jnp.dot(
                square[rest, blocks(far, reach, size)], lower_ref[:, cols], preferred_element_type=jnp.float32
            )
        result[:, cols] = (3.0 * square[rest, cols].astype(jnp.float32) - 2.0 * value).astype(result.dtype)
        low = max(low_cols, 2 * p - reach)
        high = min(far_cols, 2 * p + 2 + reach)
        if 2 * p < far_cols:
            if low < high:
                cube_ref[:, cols] = jnp.dot(
                    square[: far * size, blocks(low, high, size)],
                    panel_ref[blocks(low - reach, high - reach, size), cols],
                    preferred_element_type=jnp.float32,
                )
            else:
                cube_ref[:, cols] = jnp.zeros((far * size, 2 * size), jnp.float32)
    high_ref[...] = square[: far * size, blocks(low_cols, far_cols, size)]
    for i in range(near):
        index = jnp.where(flip == 0, i, near - 1 - i)
        for s in range(2 * half):
            place = pl.multiple_of(own_place(columns_ref, i + reach + far, s, width) * size, size)
            target = stay_ref if s < half else leave_ref
            target[index, s % half] = result[blocks(i, i + 1, size), pl.ds(place, size)]


def far_kernel(
    held_ref, mask_ref, part_ref, high_ref, cube_ref, lower_ref, panel_ref, far_ref,
    stay_ref, leave_ref, farthest, square, result, columns_ref, sem
):
    reach, far = REACH, stay_ref.shape[0]
    scalars = pltpu.make_async_copy(held_ref, columns_ref, sem)
    scalars.start()
    half, size = stay_ref.shape[1], stay_ref.shape[2]
    low_cols = reach + far
    far_cols = 2 * reach + far
    near_cols = 2 * reach
    at = 0
    for f in range(far):
        for k in range(low_cols):
            here = (blocks(f, f + 1, size), blocks(k, k + 1, size))
            if k <= f + reach:
                farthest[here] = far_ref[at]
                at += 1
            else:
                farthest[here] = jnp.zeros((size, size), farthest.dtype)
    result[:, blocks(far_cols, far_cols + 1, size)] = jnp.zeros((far * size, size), result.dtype)
    left = panel_ref[blocks(0, far, size), blocks(0, far, size)]
    for p in range(low_cols // 2):
        cols = blocks(2 * p, 2 * p + 2, size)
        value = part_ref[:, cols] + jnp.dot(left, farthest[:, cols], preferred_element_type=jnp.float32)
        for i in range(far):
            for k in (2 * p, 2 * p + 1):
                block = value[blocks(i, i + 1, size), blocks(k - 2 * p, k - 2 * p + 1, size)]
                here = (blocks(i, i + 1, size), blocks(k, k + 1, size))
                if abs(i + reach - k) <= reach:
                    mask = mask_ref[i * low_cols + k : i * low_cols + k + 1, :]
                    square[here] = jnp.where(mask > 0, block, 0.0).astype(square.dtype)
                else:
                    square[here] = jnp.zeros((size, size), square.dtype)
    for p in range(far_cols // 2):
        cols = blocks(2 * p, 2 * p + 2, size)
        value = cube_ref[:, cols] + jnp.dot(
            square[:, blocks(reach, low_cols, size)],
            panel_ref[blocks(0, far, size), cols],
            preferred_element_type=jnp.float32,
        )
        if 2 * p < near_cols:
            value = value + jnp.dot(
                square[:, blocks(far, reach, size)], lower_ref[:, cols], preferred_element_type=jnp.float32
            )
        if 2 * p < low_cols:
            value = value + jnp.dot(
                square[:, blocks(0, far, size)], farthest[:, cols], preferred_element_type=jnp.float32
            )
            kept = square[:, cols]
        else:
            kept = high_ref[:, blocks(2 * p - low_cols, 2 * p + 2 - low_cols, size)]
        result[:, cols] = (3.0 * kept.astype(jnp.float32) - 2.0 * value).astype(result.dtype)
    scalars.wait()
    for i in range(far):
        index = jnp.where(lax.axis_index("col") == 0, i, far - 1 - i)
        for s in range(2 * half):
            place = pl.multiple_of(own_place(columns_ref, i + reach, s, far_cols) * size, size)
            target = stay_ref if s < half else leave_ref
            target[index, s % half] = result[blocks(i, i + 1, size), pl.ds(place, size)]


def write_rows(pieces, out_ref, sems):
    straight = lax.axis_index("col") == 0
    copies = []
    for rows_ref, here, there in pieces:
        for n in range(rows_ref.shape[0]):
            to = out_ref.at[jnp.where(straight, here, there) + n]
            copies.append(pltpu.make_async_copy(rows_ref.at[n], to, sems.at[len(copies)]))
    for copy in copies:
        copy.start()
    for copy in copies:
        copy.wait()


def store_kernel(far_ref, near_ref, got_near_ref, out_ref, sems):
    rows, far, near = out_ref.shape[0], far_ref.shape[0], near_ref.shape[0]
    pieces = (
        (far_ref, 0, rows - far),
        (near_ref, far, rows - far - near),
        (got_near_ref, rows - far - near, far),
    )
    write_rows(pieces, out_ref, sems)


def finish_kernel(got_ref, before_ref, out_ref, sems):
    write_rows(((got_ref, out_ref.shape[0] - got_ref.shape[0], 0),), out_ref, sems)


def local(matrix, columns):
    local_rows, own_slots, size = matrix.shape[:3]
    dtype = matrix.dtype
    reach = REACH
    far = reach // 2
    near = reach - far
    cols = lax.axis_size("col")
    ring = lax.axis_size("row")
    width = local_rows + reach
    low_cols = reach + far
    far_cols = 2 * reach + far
    near_cols = 2 * reach
    same = [(r * cols, (r + 1) % ring * cols) for r in range(ring)] + [
        (r * cols + 1, (r - 1) % ring * cols + 1) for r in range(ring)
    ]
    swap = [(r * cols + 1, (r + 1) % ring * cols) for r in range(ring)] + [
        (r * cols, (r - 1) % ring * cols + 1) for r in range(ring)
    ]
    beside = [(i, (i + 1) % cols) for i in range(cols)]
    axes = ("row", "col")
    edge_rows = own_slots * size
    edges = pl.pallas_call(
        functools.partial(edge_kernel, near),
        out_shape=(
            jax.ShapeDtypeStruct((edge_rows + TILE, size), dtype),
            *[jax.ShapeDtypeStruct((edge_rows, size), dtype)] * (2 * near - 1),
            jax.ShapeDtypeStruct(columns.shape, columns.dtype),
        ),
        in_specs=[HBM, HBM],
        out_specs=(VMEM,) * (2 * near + 1),
        scratch_shapes=[pltpu.VMEM((TILE, size), jnp.float32), pltpu.SemaphoreType.DMA((3,))],
        compiler_params=limit(1),
        cost_estimate=LIGHT,
        name="edge",
    )(
        pltpu.with_memory_space_constraint(columns, pltpu.HBM),
        pltpu.with_memory_space_constraint(matrix, pltpu.HBM),
    )
    held = edges[-1]
    near_rows, cross_rows = [], []
    for n in range(near):
        near_rows.append(lax.ppermute(edges[n], axes, same))
        cross_rows.append(lax.ppermute(edges[near + n], axes, swap))
    other = lax.ppermute(matrix, "col", beside)

    panel, first_part = pl.pallas_call(
        functools.partial(base_kernel, far),
        out_shape=(
            jax.ShapeDtypeStruct((local_rows * size, (width + 1) * size), dtype),
            jax.ShapeDtypeStruct((reach * size, width * size), jnp.float32),
        ),
        in_specs=[SMEM, VMEM, VMEM],
        out_specs=(VMEM, VMEM),
        compiler_params=limit(12),
        cost_estimate=LIGHT,
        name="base",
    )(held, matrix, other)
    packed = pl.pallas_call(
        functools.partial(pack_kernel, far),
        out_shape=jax.ShapeDtypeStruct((sum(reach + 1 + f for f in range(far)), size, size), dtype),
        in_specs=[VMEM, ANY],
        out_specs=VMEM,
        compiler_params=limit(1),
        cost_estimate=LIGHT,
        name="pack",
    )(panel, held)
    far_blocks = lax.ppermute(packed, axes, swap)

    rows_out = jax.ShapeDtypeStruct((near, own_slots, size, size), dtype)
    stay_near, leave_near, mask, part, high, cube, lower = pl.pallas_call(
        functools.partial(near_kernel, far),
        out_shape=(
            rows_out,
            rows_out,
            jax.ShapeDtypeStruct((far * low_cols, size), jnp.float32),
            jax.ShapeDtypeStruct((far * size, low_cols * size), jnp.float32),
            jax.ShapeDtypeStruct((far * size, (far_cols - low_cols) * size), dtype),
            jax.ShapeDtypeStruct((far * size, far_cols * size), jnp.float32),
            jax.ShapeDtypeStruct((near * size, (near_cols + 1) * size), dtype),
        ),
        in_specs=[VMEM] * (3 + 2 * near),
        out_specs=(VMEM,) * 7,
        scratch_shapes=[
            pltpu.VMEM((reach * size, width * size), dtype),
            pltpu.VMEM((near * size, (width + 1) * size), dtype),
            pltpu.SMEM((reach, width + 1), jnp.int32),
            pltpu.SMEM(columns.shape, columns.dtype),
            pltpu.VMEM((TILE, size), jnp.int32),
            pltpu.SMEM((TILE, size), jnp.int32),
            pltpu.SemaphoreType.DMA((2,)),
        ],
        compiler_params=limit(16),
        cost_estimate=HEAVY,
        name="near",
    )(held, panel, first_part, *near_rows, *cross_rows)
    arrived_near = lax.ppermute(leave_near, "col", beside)

    far_out = jax.ShapeDtypeStruct((far, own_slots, size, size), dtype)
    stay_far, leave_far = pl.pallas_call(
        far_kernel,
        out_shape=(far_out, far_out),
        in_specs=[VMEM] * 8,
        out_specs=(VMEM, VMEM),
        scratch_shapes=[
            pltpu.VMEM((far * size, low_cols * size), dtype),
            pltpu.VMEM((far * size, low_cols * size), dtype),
            pltpu.VMEM((far * size, (far_cols + 1) * size), dtype),
            pltpu.SMEM(columns.shape, columns.dtype),
            pltpu.SemaphoreType.DMA,
        ],
        compiler_params=limit(16),
        cost_estimate=LIGHT,
        name="far",
    )(held, mask, part, high, cube, lower, panel, far_blocks)
    arrived_far = lax.ppermute(leave_far, "col", beside)
    out = pl.pallas_call(
        store_kernel,
        out_shape=jax.ShapeDtypeStruct(matrix.shape, dtype),
        in_specs=[VMEM] * 3,
        out_specs=HBM,
        scratch_shapes=[pltpu.SemaphoreType.DMA((far + 2 * near,))],
        compiler_params=limit(1),
        cost_estimate=LIGHT,
        name="store",
    )(stay_far, stay_near, arrived_near)
    return pl.pallas_call(
        finish_kernel,
        out_shape=jax.ShapeDtypeStruct(matrix.shape, dtype),
        in_specs=[VMEM, HBM],
        out_specs=HBM,
        input_output_aliases={1: 0},
        scratch_shapes=[pltpu.SemaphoreType.DMA((far,))],
        compiler_params=limit(1),
        cost_estimate=LIGHT,
        name="finish",
    )(arrived_far, out)


def solution(mesh):
    placed = (P(("geom", "row"), "col", None, None), P("row", None))
    return jax.shard_map(
        local,
        mesh=mesh,
        in_specs=placed,
        out_specs=P(("geom", "row"), "col", None, None),
        check_vma=False,
    )
```

```python
import functools

import jax
import jax.numpy as jnp
from jax import lax
from jax.experimental import pallas as pl
from jax.experimental.pallas import tpu as pltpu
from jax.sharding import PartitionSpec as P

REACH = 4
HEAD = 1
MIB = 1024 * 1024
ABSENT = 64
TILE = 16

HEAVY = pl.CostEstimate(flops=20_000_000_000, bytes_accessed=0, transcendentals=0)
LIGHT = pl.CostEstimate(flops=0, bytes_accessed=0, transcendentals=0)

SMEM = pl.BlockSpec(memory_space=pltpu.SMEM)
VMEM = pl.BlockSpec(memory_space=pltpu.VMEM)
ANY = pl.BlockSpec(memory_space=pl.ANY)
HBM = pl.BlockSpec(memory_space=pltpu.HBM)


def limit(mib):
    return pltpu.CompilerParams(vmem_limit_bytes=mib * MIB)


def blocks(first, last, size):
    return slice(first * size, last * size)


def own_place(columns_ref, q, s, limit):
    rows, slots = columns_ref.shape
    flip = lax.axis_index("col")
    row = jnp.where(flip == 0, q - REACH, rows + REACH - 1 - q)
    slot = lax.rem(s + flip * (slots // 2), slots)
    total = rows * lax.axis_size("row")
    column = columns_ref[row, slot]
    step = column - lax.axis_index("row") * rows - row
    step = jnp.where(step > REACH, step - total, step)
    step = jnp.where(step < -REACH, step + total, step)
    place = jnp.where(flip == 0, q + step, q - step)
    inside = (column >= 0) & (place >= 0) & (place < limit)
    return jnp.where(inside, place, limit)


def halo_place(steps_ref, rows, slots, q, s, limit):
    flip = lax.axis_index("col")
    row = jnp.where(flip == 0, rows - REACH + q, REACH - 1 - q)
    slot = lax.rem(s + flip * (slots // 2), slots)
    step = steps_ref[row, slot]
    place = jnp.where(flip == 0, q + step, q - step)
    inside = (step <= REACH) & (place >= 0) & (place < limit)
    return jnp.where(inside, place, limit)


def edge_kernel(near, columns_ref, matrix_ref, *refs):
    rows, half, size = matrix_ref.shape[:3]
    same_refs, swap_refs = refs[:near], refs[near : 2 * near]
    copied_ref, steps, sems = refs[2 * near :]
    straight = lax.axis_index("col") == 0
    copies = []
    for n in range(near):
        up, down = rows - 1 - n, n
        for s in range(half):
            at = blocks(s, s + 1, size)
            source = matrix_ref.at[jnp.where(straight, up, down), s]
            copies.append(pltpu.make_async_copy(source, same_refs[n].at[at], sems.at[0]))
            source = matrix_ref.at[jnp.where(straight, down, up), s]
            copies.append(pltpu.make_async_copy(source, swap_refs[n].at[at], sems.at[1]))
    held = pltpu.make_async_copy(columns_ref, copied_ref, sems.at[2])
    held.start()
    for copy in copies:
        copy.start()
    held.wait()
    column = copied_ref[...]
    row = lax.broadcasted_iota(jnp.int32, column.shape, 0) + lax.axis_index("row") * rows
    total = rows * lax.axis_size("row")
    step = column - row
    step = jnp.where(step > REACH, step - total, step)
    step = jnp.where(step < -REACH, step + total, step)
    step = jnp.where(column >= 0, step, ABSENT)
    steps[...] = jnp.zeros_like(steps)
    steps[:rows, : column.shape[1]] = step.astype(jnp.float32)
    same_refs[0][half * size :, :] = steps[...].astype(same_refs[0].dtype)
    for copy in copies:
        copy.wait()


def pack_kernel(far, held_ref, matrix_ref, other_ref, mid_ref, last_ref, own, columns_ref, sems):
    rows, half = other_ref.shape[:2]
    lead = own.shape[0]
    straight = lax.axis_index("col") == 0
    start = jnp.where(straight, REACH - lead, rows - REACH)
    copies = [
        pltpu.make_async_copy(held_ref, columns_ref, sems.at[0]),
        pltpu.make_async_copy(matrix_ref.at[pl.ds(start, lead)], own, sems.at[1]),
    ]
    for copy in copies:
        copy.start()
    mid_ref[...] = jnp.zeros_like(mid_ref)
    last_ref[...] = jnp.zeros_like(last_ref)
    for copy in copies:
        copy.wait()
    base = 0
    for f in range(lead):
        if f == far:
            base = 0
        out_ref = last_ref if f < far else mid_ref
        q = 2 * REACH - 1 - f
        index = jnp.where(straight, lead - 1 - f, f)
        count = REACH + 1 + f
        for s in range(2 * half):
            place = 2 * REACH - 1 - own_place(columns_ref, q, s, 2 * REACH + 1)

            @pl.when((place >= 0) & (place < count))
            def _(place=place, index=index, s=s, base=base, out_ref=out_ref):
                if s < half:
                    out_ref[base + place] = own[index, s]
                else:
                    out_ref[base + place] = other_ref[start + index, s - half]
        base += count


def base_kernel(
    held_ref, matrix_ref, other_ref, same_ref, swap_ref, panel_ref, first_ref, mask_ref,
    own_ref, columns_ref, keep_ref, steps, halo_ref, sems
):
    rows, half, size = own_ref.shape[0], own_ref.shape[1], own_ref.shape[2]
    reach = REACH
    width = rows + reach
    lead = reach - HEAD
    steps[...] = same_ref[half * size :, :].astype(jnp.float32).astype(jnp.int32)
    copies = [
        pltpu.make_async_copy(held_ref, columns_ref, sems.at[0]),
        pltpu.make_async_copy(steps, halo_ref, sems.at[1]),
        pltpu.make_async_copy(matrix_ref, own_ref, sems.at[2]),
    ]
    for copy in copies:
        copy.start()
    panel_ref[...] = jnp.zeros_like(panel_ref)
    for copy in copies:
        copy.wait()
    for s in range(2 * half):
        place = halo_place(halo_ref, rows, 2 * half, lead, s, width)
        place = pl.multiple_of(place * size, size)
        source = same_ref if s < half else swap_ref
        panel_ref[blocks(lead, lead + 1, size), pl.ds(place, size)] = source[
            blocks(s % half, s % half + 1, size), :
        ]
    for q in range(reach, width):
        index = jnp.where(lax.axis_index("col") == 0, q - reach, width - 1 - q)
        for s in range(2 * half):
            place = pl.multiple_of(own_place(columns_ref, q, s, width) * size, size)
            source = own_ref if s < half else other_ref
            panel_ref[blocks(q, q + 1, size), pl.ds(place, size)] = source[index, s % half]
    for i in range(reach):
        for k in range(width + 1):
            keep_ref[i, k] = 0
        for s in range(2 * half):
            keep_ref[i, own_place(columns_ref, i + reach, s, width)] = 1
        for k in range(width):
            at = i * width + k
            mask_ref[at : at + 1, :] = jnp.full((1, size), keep_ref[i, k], jnp.float32)
    for p in range(width // 2):
        low = max(lead, 2 * p - reach)
        high = min(width, 2 * p + 2 + reach)
        cols = blocks(2 * p, 2 * p + 2, size)
        first_ref[:, cols] = jnp.dot(
            panel_ref[blocks(reach, 2 * reach, size), blocks(low, high, size)],
            panel_ref[blocks(low, high, size), cols],
            preferred_element_type=jnp.float32,
        )


def keep_block(mask_ref, i, k, width, block, dtype):
    if abs(i + REACH - k) > REACH:
        return jnp.zeros(block.shape, dtype)
    return jnp.where(mask_ref[i * width + k : i * width + k + 1, :] > 0, block, 0.0).astype(dtype)


def near_kernel(
    far, held_ref, mask_ref, first_ref, mid_ref, before_ref,
    panel_ref, stay_ref, leave_ref, part_ref, high_ref, cube_ref, square, result, columns_ref, sem
):
    reach = REACH
    lead = reach - HEAD
    scalars = pltpu.make_async_copy(held_ref, columns_ref, sem)
    scalars.start()
    half, size = stay_ref.shape[1], stay_ref.shape[2]
    width = panel_ref.shape[0] // size
    near = reach - far
    low_cols = reach + far
    far_cols = 2 * reach + far
    near_cols = 2 * reach
    at = 0
    for q in range(far, lead):
        for k in range(reach + 1 + q):
            panel_ref[blocks(q, q + 1, size), blocks(k, k + 1, size)] = mid_ref[at]
            at += 1
    result[:, blocks(width, width + 1, size)] = jnp.zeros((near * size, size), result.dtype)
    left = panel_ref[blocks(reach, 2 * reach, size), blocks(far, lead, size)]
    for p in range(width // 2):
        cols = blocks(2 * p, 2 * p + 2, size)
        value = first_ref[:, cols]
        if 2 * p < near_cols:
            value = value + jnp.dot(
                left, panel_ref[blocks(far, lead, size), cols], preferred_element_type=jnp.float32
            )
        for i in range(reach):
            for k in (2 * p, 2 * p + 1):
                block = value[blocks(i, i + 1, size), blocks(k - 2 * p, k - 2 * p + 1, size)]
                here = (blocks(i, i + 1, size), blocks(k, k + 1, size))
                if i < far and k < low_cols:
                    part_ref[here] = block
                    square[here] = jnp.zeros((size, size), square.dtype)
                else:
                    square[here] = keep_block(mask_ref, i, k, width, block, square.dtype)
    rest = slice(far * size, reach * size)
    for p in range(width // 2):
        cols = blocks(2 * p, 2 * p + 2, size)
        low = max(far, 2 * p - reach)
        high = min(width, 2 * p + 2 + reach)
        value = jnp.dot(
            square[rest, blocks(low, high, size)],
            panel_ref[blocks(low, high, size), cols],
            preferred_element_type=jnp.float32,
        )
        result[:, cols] = (3.0 * square[rest, cols].astype(jnp.float32) - 2.0 * value).astype(result.dtype)
        low = max(low_cols, 2 * p - reach)
        high = min(far_cols, 2 * p + 2 + reach)
        if 2 * p < far_cols:
            if low < high:
                cube_ref[:, cols] = jnp.dot(
                    square[: far * size, blocks(low, high, size)],
                    panel_ref[blocks(low, high, size), cols],
                    preferred_element_type=jnp.float32,
                )
            else:
                cube_ref[:, cols] = jnp.zeros((far * size, 2 * size), jnp.float32)
    high_ref[...] = square[: far * size, blocks(low_cols, far_cols, size)]
    scalars.wait()
    for i in range(near):
        index = jnp.where(lax.axis_index("col") == 0, i, near - 1 - i)
        for s in range(2 * half):
            place = pl.multiple_of(own_place(columns_ref, i + reach + far, s, width) * size, size)
            target = stay_ref if s < half else leave_ref
            target[index, s % half] = result[blocks(i, i + 1, size), pl.ds(place, size)]


def far_kernel(
    held_ref, mask_ref, part_ref, high_ref, cube_ref, far_ref, before_ref,
    panel_ref, stay_ref, leave_ref, square, result, columns_ref, sem
):
    reach, far = REACH, stay_ref.shape[0]
    scalars = pltpu.make_async_copy(held_ref, columns_ref, sem)
    scalars.start()
    half, size = stay_ref.shape[1], stay_ref.shape[2]
    width = panel_ref.shape[0] // size
    low_cols = reach + far
    far_cols = 2 * reach + far
    at = 0
    for f in range(far):
        for k in range(reach + 1 + f):
            panel_ref[blocks(f, f + 1, size), blocks(k, k + 1, size)] = far_ref[at]
            at += 1
    result[:, blocks(far_cols, far_cols + 1, size)] = jnp.zeros((far * size, size), result.dtype)
    left = panel_ref[blocks(reach, reach + far, size), blocks(0, far, size)]
    for p in range(low_cols // 2):
        cols = blocks(2 * p, 2 * p + 2, size)
        value = part_ref[:, cols] + jnp.dot(
            left, panel_ref[blocks(0, far, size), cols], preferred_element_type=jnp.float32
        )
        for i in range(far):
            for k in (2 * p, 2 * p + 1):
                block = value[blocks(i, i + 1, size), blocks(k - 2 * p, k - 2 * p + 1, size)]
                here = (blocks(i, i + 1, size), blocks(k, k + 1, size))
                square[here] = keep_block(mask_ref, i, k, width, block, square.dtype)
    for p in range(far_cols // 2):
        cols = blocks(2 * p, 2 * p + 2, size)
        low = max(0, 2 * p - reach)
        value = cube_ref[:, cols] + jnp.dot(
            square[:, blocks(low, low_cols, size)],
            panel_ref[blocks(low, low_cols, size), cols],
            preferred_element_type=jnp.float32,
        )
        if 2 * p < low_cols:
            kept = square[:, cols]
        else:
            kept = high_ref[:, blocks(2 * p - low_cols, 2 * p + 2 - low_cols, size)]
        result[:, cols] = (3.0 * kept.astype(jnp.float32) - 2.0 * value).astype(result.dtype)
    scalars.wait()
    for i in range(far):
        index = jnp.where(lax.axis_index("col") == 0, i, far - 1 - i)
        for s in range(2 * half):
            place = pl.multiple_of(own_place(columns_ref, i + reach, s, far_cols) * size, size)
            target = stay_ref if s < half else leave_ref
            target[index, s % half] = result[blocks(i, i + 1, size), pl.ds(place, size)]


def write_rows(pieces, out_ref, sems):
    straight = lax.axis_index("col") == 0
    copies = []
    for rows_ref, here, there in pieces:
        for n in range(rows_ref.shape[0]):
            to = out_ref.at[jnp.where(straight, here, there) + n]
            copies.append(pltpu.make_async_copy(rows_ref.at[n], to, sems.at[len(copies)]))
    for copy in copies:
        copy.start()
    for copy in copies:
        copy.wait()


def store_kernel(far_ref, near_ref, got_near_ref, out_ref, sems):
    rows, far, near = out_ref.shape[0], far_ref.shape[0], near_ref.shape[0]
    pieces = (
        (far_ref, 0, rows - far),
        (near_ref, far, rows - far - near),
        (got_near_ref, rows - far - near, far),
    )
    write_rows(pieces, out_ref, sems)


def finish_kernel(got_ref, before_ref, out_ref, sems):
    write_rows(((got_ref, out_ref.shape[0] - got_ref.shape[0], 0),), out_ref, sems)


def local(matrix, columns):
    local_rows, own_slots, size = matrix.shape[:3]
    dtype = matrix.dtype
    reach = REACH
    far = reach // 2
    near = reach - far
    cols = lax.axis_size("col")
    ring = lax.axis_size("row")
    width = local_rows + reach
    low_cols = reach + far
    far_cols = 2 * reach + far
    same = [(r * cols, (r + 1) % ring * cols) for r in range(ring)] + [
        (r * cols + 1, (r - 1) % ring * cols + 1) for r in range(ring)
    ]
    swap = [(r * cols + 1, (r + 1) % ring * cols) for r in range(ring)] + [
        (r * cols, (r - 1) % ring * cols + 1) for r in range(ring)
    ]
    beside = [(i, (i + 1) % cols) for i in range(cols)]
    axes = ("row", "col")
    edge_rows = own_slots * size
    in_place = pltpu.with_memory_space_constraint(matrix, pltpu.HBM)
    same_edge, swap_edge, held = pl.pallas_call(
        functools.partial(edge_kernel, HEAD),
        out_shape=(
            jax.ShapeDtypeStruct((edge_rows + TILE, size), dtype),
            jax.ShapeDtypeStruct((edge_rows, size), dtype),
            jax.ShapeDtypeStruct(columns.shape, columns.dtype),
        ),
        in_specs=[HBM, HBM],
        out_specs=(VMEM,) * 3,
        scratch_shapes=[pltpu.VMEM((TILE, size), jnp.float32), pltpu.SemaphoreType.DMA((3,))],
        compiler_params=limit(1),
        cost_estimate=LIGHT,
        name="edge",
    )(pltpu.with_memory_space_constraint(columns, pltpu.HBM), in_place)
    same_rows = lax.ppermute(same_edge, axes, same)
    swap_rows = lax.ppermute(swap_edge, axes, swap)
    other = lax.ppermute(matrix, "col", beside)

    lead = reach - HEAD
    scalars = pltpu.SMEM(columns.shape, columns.dtype)
    packed_mid, packed_last = pl.pallas_call(
        functools.partial(pack_kernel, far),
        out_shape=tuple(
            jax.ShapeDtypeStruct((sum(reach + 1 + f for f in part), size, size), dtype)
            for part in (range(far, lead), range(far))
        ),
        in_specs=[VMEM, HBM, VMEM],
        out_specs=(VMEM, VMEM),
        scratch_shapes=[
            pltpu.VMEM((lead,) + matrix.shape[1:], dtype),
            scalars,
            pltpu.SemaphoreType.DMA((2,)),
        ],
        compiler_params=limit(2),
        cost_estimate=LIGHT,
        name="pack",
    )(held, in_place, other)
    mid_blocks = lax.ppermute(packed_mid, axes, swap)
    far_blocks = lax.ppermute(packed_last, axes, swap)

    panel_shape = jax.ShapeDtypeStruct((width * size, (width + 1) * size), dtype)
    panel, first_part, mask = pl.pallas_call(
        base_kernel,
        out_shape=(
            panel_shape,
            jax.ShapeDtypeStruct((reach * size, width * size), jnp.float32),
            jax.ShapeDtypeStruct((reach * width, size), jnp.float32),
        ),
        in_specs=[VMEM, HBM, VMEM, VMEM, VMEM],
        out_specs=(VMEM,) * 3,
        scratch_shapes=[
            pltpu.VMEM(matrix.shape, dtype),
            scalars,
            pltpu.SMEM((reach, width + 1), jnp.int32),
            pltpu.VMEM((TILE, size), jnp.int32),
            pltpu.SMEM((TILE, size), jnp.int32),
            pltpu.SemaphoreType.DMA((3,)),
        ],
        compiler_params=limit(12),
        cost_estimate=HEAVY,
        name="base",
    )(held, in_place, other, same_rows, swap_rows)

    rows_out = jax.ShapeDtypeStruct((near, own_slots, size, size), dtype)
    panel, stay_near, leave_near, part, high, cube = pl.pallas_call(
        functools.partial(near_kernel, far),
        out_shape=(
            panel_shape,
            rows_out,
            rows_out,
            jax.ShapeDtypeStruct((far * size, low_cols * size), jnp.float32),
            jax.ShapeDtypeStruct((far * size, (far_cols - low_cols) * size), dtype),
            jax.ShapeDtypeStruct((far * size, far_cols * size), jnp.float32),
        ),
        in_specs=[VMEM] * 5,
        out_specs=(VMEM,) * 6,
        input_output_aliases={4: 0},
        scratch_shapes=[
            pltpu.VMEM((reach * size, width * size), dtype),
            pltpu.VMEM((near * size, (width + 1) * size), dtype),
            scalars,
            pltpu.SemaphoreType.DMA,
        ],
        compiler_params=limit(16),
        cost_estimate=HEAVY,
        name="near",
    )(held, mask, first_part, mid_blocks, panel)
    arrived_near = lax.ppermute(leave_near, "col", beside)

    far_out = jax.ShapeDtypeStruct((far, own_slots, size, size), dtype)
    panel, stay_far, leave_far = pl.pallas_call(
        far_kernel,
        out_shape=(panel_shape, far_out, far_out),
        in_specs=[VMEM] * 7,
        out_specs=(VMEM,) * 3,
        input_output_aliases={6: 0},
        scratch_shapes=[
            pltpu.VMEM((far * size, low_cols * size), dtype),
            pltpu.VMEM((far * size, (far_cols + 1) * size), dtype),
            scalars,
            pltpu.SemaphoreType.DMA,
        ],
        compiler_params=limit(16),
        cost_estimate=LIGHT,
        name="far",
    )(held, mask, part, high, cube, far_blocks, panel)
    arrived_far = lax.ppermute(leave_far, "col", beside)
    out = pl.pallas_call(
        store_kernel,
        out_shape=jax.ShapeDtypeStruct(matrix.shape, dtype),
        in_specs=[VMEM] * 3,
        out_specs=HBM,
        scratch_shapes=[pltpu.SemaphoreType.DMA((far + 2 * near,))],
        compiler_params=limit(1),
        cost_estimate=LIGHT,
        name="store",
    )(stay_far, stay_near, arrived_near)
    return pl.pallas_call(
        finish_kernel,
        out_shape=jax.ShapeDtypeStruct(matrix.shape, dtype),
        in_specs=[VMEM, HBM],
        out_specs=HBM,
        input_output_aliases={1: 0},
        scratch_shapes=[pltpu.SemaphoreType.DMA((far,))],
        compiler_params=limit(1),
        cost_estimate=LIGHT,
        name="finish",
    )(arrived_far, out)


def solution(mesh):
    placed = (P(("geom", "row"), "col", None, None), P("row", None))
    return jax.shard_map(
        local,
        mesh=mesh,
        in_specs=placed,
        out_specs=P(("geom", "row"), "col", None, None),
        check_vma=False,
    )
```

```python
import functools

import jax
import jax.numpy as jnp
from jax import lax
from jax.experimental import pallas as pl
from jax.experimental.pallas import tpu as pltpu
from jax.sharding import PartitionSpec as P

REACH = 4
HEAD = 1
MIB = 1024 * 1024
ABSENT = 64
TILE = 16

HEAVY = pl.CostEstimate(flops=20_000_000_000, bytes_accessed=0, transcendentals=0)
LIGHT = pl.CostEstimate(flops=0, bytes_accessed=0, transcendentals=0)
SHORT = pl.CostEstimate(flops=500_000_000, bytes_accessed=0, transcendentals=0)
MEDIUM = pl.CostEstimate(flops=1_200_000_000, bytes_accessed=0, transcendentals=0)

SMEM = pl.BlockSpec(memory_space=pltpu.SMEM)
VMEM = pl.BlockSpec(memory_space=pltpu.VMEM)
ANY = pl.BlockSpec(memory_space=pl.ANY)
HBM = pl.BlockSpec(memory_space=pltpu.HBM)


def limit(mib):
    return pltpu.CompilerParams(vmem_limit_bytes=mib * MIB)


def blocks(first, last, size):
    return slice(first * size, last * size)


def own_place(columns_ref, q, s, limit):
    rows, slots = columns_ref.shape
    flip = lax.axis_index("col")
    row = jnp.where(flip == 0, q - REACH, rows + REACH - 1 - q)
    slot = lax.rem(s + flip * (slots // 2), slots)
    total = rows * lax.axis_size("row")
    column = columns_ref[row, slot]
    step = column - lax.axis_index("row") * rows - row
    step = jnp.where(step > REACH, step - total, step)
    step = jnp.where(step < -REACH, step + total, step)
    place = jnp.where(flip == 0, q + step, q - step)
    inside = (column >= 0) & (place >= 0) & (place < limit)
    return jnp.where(inside, place, limit)


def halo_place(steps_ref, rows, slots, q, s, limit):
    flip = lax.axis_index("col")
    row = jnp.where(flip == 0, rows - REACH + q, REACH - 1 - q)
    slot = lax.rem(s + flip * (slots // 2), slots)
    step = steps_ref[row, slot]
    place = jnp.where(flip == 0, q + step, q - step)
    inside = (step <= REACH) & (place >= 0) & (place < limit)
    return jnp.where(inside, place, limit)


def edge_kernel(near, columns_ref, matrix_ref, *refs):
    rows, half, size = matrix_ref.shape[:3]
    same_refs, swap_refs = refs[:near], refs[near : 2 * near]
    copied_ref, steps, sems = refs[2 * near :]
    straight = lax.axis_index("col") == 0
    copies = []
    for n in range(near):
        up, down = rows - 1 - n, n
        for s in range(half):
            at = blocks(s, s + 1, size)
            source = matrix_ref.at[jnp.where(straight, up, down), s]
            copies.append(pltpu.make_async_copy(source, same_refs[n].at[at], sems.at[0]))
            source = matrix_ref.at[jnp.where(straight, down, up), s]
            copies.append(pltpu.make_async_copy(source, swap_refs[n].at[at], sems.at[1]))
    held = pltpu.make_async_copy(columns_ref, copied_ref, sems.at[2])
    held.start()
    for copy in copies:
        copy.start()
    held.wait()
    column = copied_ref[...]
    row = lax.broadcasted_iota(jnp.int32, column.shape, 0) + lax.axis_index("row") * rows
    total = rows * lax.axis_size("row")
    step = column - row
    step = jnp.where(step > REACH, step - total, step)
    step = jnp.where(step < -REACH, step + total, step)
    step = jnp.where(column >= 0, step, ABSENT)
    steps[...] = jnp.zeros_like(steps)
    steps[:rows, : column.shape[1]] = step.astype(jnp.float32)
    same_refs[0][half * size :, :] = steps[...].astype(same_refs[0].dtype)
    for copy in copies:
        copy.wait()


def pack_kernel(held_ref, matrix_ref, other_ref, after_ref, *refs):
    out_refs, (own, columns_ref, sems) = refs[:-3], refs[-3:]
    rows, half = other_ref.shape[:2]
    lead = own.shape[0]
    straight = lax.axis_index("col") == 0
    start = jnp.where(straight, REACH - lead, rows - REACH)
    copies = [
        pltpu.make_async_copy(held_ref, columns_ref, sems.at[0]),
        pltpu.make_async_copy(matrix_ref.at[pl.ds(start, lead)], own, sems.at[1]),
    ]
    for copy in copies:
        copy.start()
    for out_ref in out_refs:
        out_ref[...] = jnp.zeros_like(out_ref)
    for copy in copies:
        copy.wait()
    for f, out_ref in enumerate(out_refs):
        q = 2 * REACH - 1 - f
        index = jnp.where(straight, lead - 1 - f, f)
        count = REACH + 1 + f
        for s in range(2 * half):
            place = 2 * REACH - 1 - own_place(columns_ref, q, s, 2 * REACH + 1)

            @pl.when((place >= 0) & (place < count))
            def _(place=place, index=index, s=s, out_ref=out_ref):
                if s < half:
                    out_ref[place] = own[index, s]
                else:
                    out_ref[place] = other_ref[start + index, s - half]


def base_kernel(turn, held_ref, matrix_ref, other_ref, *refs):
    panel_ref, first_ref, mask_ref, own_ref, columns_ref, keep_ref, sems = refs[-7:]
    rows, half, size = own_ref.shape[0], own_ref.shape[1], own_ref.shape[2]
    reach = REACH
    width = rows + reach

    @pl.when(lax.rem(lax.axis_index("row") + lax.axis_index("col"), 2) == turn)
    def _():
        copies = [
            pltpu.make_async_copy(held_ref, columns_ref, sems.at[0]),
            pltpu.make_async_copy(matrix_ref, own_ref, sems.at[1]),
        ]
        for copy in copies:
            copy.start()
        panel_ref[...] = jnp.zeros_like(panel_ref)
        for copy in copies:
            copy.wait()
        for q in range(reach, width):
            index = jnp.where(lax.axis_index("col") == 0, q - reach, width - 1 - q)
            for s in range(2 * half):
                place = pl.multiple_of(own_place(columns_ref, q, s, width) * size, size)
                source = own_ref if s < half else other_ref
                panel_ref[blocks(q, q + 1, size), pl.ds(place, size)] = source[index, s % half]
        for i in range(reach):
            for k in range(width + 1):
                keep_ref[i, k] = 0
            for s in range(2 * half):
                keep_ref[i, own_place(columns_ref, i + reach, s, width)] = 1
            for k in range(width):
                at = i * width + k
                mask_ref[at : at + 1, :] = jnp.full((1, size), keep_ref[i, k], jnp.float32)
        for p in range(width // 2):
            low = max(reach, 2 * p - reach)
            high = min(width, 2 * p + 2 + reach)
            cols = blocks(2 * p, 2 * p + 2, size)
            first_ref[:, cols] = jnp.dot(
                panel_ref[blocks(reach, 2 * reach, size), blocks(low, high, size)],
                panel_ref[blocks(low, high, size), cols],
                preferred_element_type=jnp.float32,
            )


def lead_kernel(
    half, same_ref, swap_ref, before_panel, before_first, panel_ref, first_ref, steps, halo_ref, sem
):
    size = same_ref.shape[1]
    reach = REACH
    width = panel_ref.shape[0] // size
    lead = reach - HEAD
    steps[...] = same_ref[half * size :, :].astype(jnp.float32).astype(jnp.int32)
    copy = pltpu.make_async_copy(steps, halo_ref, sem)
    copy.start()
    copy.wait()
    for s in range(2 * half):
        place = halo_place(halo_ref, width - reach, 2 * half, lead, s, width)
        place = pl.multiple_of(place * size, size)
        source = same_ref if s < half else swap_ref
        panel_ref[blocks(lead, lead + 1, size), pl.ds(place, size)] = source[
            blocks(s % half, s % half + 1, size), :
        ]
    left = panel_ref[blocks(reach, 2 * reach, size), blocks(lead, reach, size)]
    for p in range(reach):
        cols = blocks(2 * p, 2 * p + 2, size)
        first_ref[:, cols] += jnp.dot(
            left, panel_ref[blocks(lead, reach, size), cols], preferred_element_type=jnp.float32
        )


def keep_block(mask_ref, i, k, width, block, dtype):
    if abs(i + REACH - k) > REACH:
        return jnp.zeros(block.shape, dtype)
    return jnp.where(mask_ref[i * width + k : i * width + k + 1, :] > 0, block, 0.0).astype(dtype)


def near_kernel(
    far, held_ref, mask_ref, first_ref, before_ref, *refs
):
    mid_refs = refs[: REACH - HEAD - far]
    (
        panel_ref, stay_ref, leave_ref, part_ref, high_ref, cube_ref, square, result, columns_ref, sem,
    ) = refs[REACH - HEAD - far :]
    reach = REACH
    lead = reach - HEAD
    scalars = pltpu.make_async_copy(held_ref, columns_ref, sem)
    scalars.start()
    half, size = stay_ref.shape[1], stay_ref.shape[2]
    width = panel_ref.shape[0] // size
    near = reach - far
    low_cols = reach + far
    far_cols = 2 * reach + far
    near_cols = 2 * reach
    for q, mid_ref in zip(range(far, lead), mid_refs):
        for k in range(reach + 1 + q):
            panel_ref[blocks(q, q + 1, size), blocks(k, k + 1, size)] = mid_ref[k]
    result[:, blocks(width, width + 1, size)] = jnp.zeros((near * size, size), result.dtype)
    left = panel_ref[blocks(reach, 2 * reach, size), blocks(far, lead, size)]
    for p in range(width // 2):
        cols = blocks(2 * p, 2 * p + 2, size)
        value = first_ref[:, cols]
        if 2 * p < near_cols:
            value = value + jnp.dot(
                left, panel_ref[blocks(far, lead, size), cols], preferred_element_type=jnp.float32
            )
        for i in range(reach):
            for k in (2 * p, 2 * p + 1):
                block = value[blocks(i, i + 1, size), blocks(k - 2 * p, k - 2 * p + 1, size)]
                here = (blocks(i, i + 1, size), blocks(k, k + 1, size))
                if i < far and k < low_cols:
                    part_ref[here] = block
                    square[here] = jnp.zeros((size, size), square.dtype)
                else:
                    square[here] = keep_block(mask_ref, i, k, width, block, square.dtype)
    rest = slice(far * size, reach * size)
    for p in range(width // 2):
        cols = blocks(2 * p, 2 * p + 2, size)
        low = max(far, 2 * p - reach)
        high = min(width, 2 * p + 2 + reach)
        value = jnp.dot(
            square[rest, blocks(low, high, size)],
            panel_ref[blocks(low, high, size), cols],
            preferred_element_type=jnp.float32,
        )
        result[:, cols] = (3.0 * square[rest, cols].astype(jnp.float32) - 2.0 * value).astype(result.dtype)
        low = max(low_cols, 2 * p - reach)
        high = min(far_cols, 2 * p + 2 + reach)
        if 2 * p < far_cols:
            if low < high:
                cube_ref[:, cols] = jnp.dot(
                    square[: far * size, blocks(low, high, size)],
                    panel_ref[blocks(low, high, size), cols],
                    preferred_element_type=jnp.float32,
                )
            else:
                cube_ref[:, cols] = jnp.zeros((far * size, 2 * size), jnp.float32)
    high_ref[...] = square[: far * size, blocks(low_cols, far_cols, size)]
    scalars.wait()
    for i in range(near):
        index = jnp.where(lax.axis_index("col") == 0, i, near - 1 - i)
        for s in range(2 * half):
            place = pl.multiple_of(own_place(columns_ref, i + reach + far, s, width) * size, size)
            target = stay_ref if s < half else leave_ref
            target[index, s % half] = result[blocks(i, i + 1, size), pl.ds(place, size)]


def far_kernel(
    far, i, held_ref, mask_ref, part_ref, high_ref, cube_ref, row_ref, before_ref,
    panel_ref, stay_ref, leave_ref, square, result, columns_ref, sem
):
    reach = REACH
    scalars = pltpu.make_async_copy(held_ref, columns_ref, sem)
    scalars.start()
    half, size = stay_ref.shape[1], stay_ref.shape[2]
    width = panel_ref.shape[0] // size
    low_cols = reach + far
    far_cols = 2 * reach + far
    mine = blocks(i, i + 1, size)
    for k in range(reach + 1 + i):
        panel_ref[mine, blocks(k, k + 1, size)] = row_ref[k]
    result[:, blocks(far_cols, far_cols + 1, size)] = jnp.zeros((size, size), result.dtype)
    left = panel_ref[blocks(reach + i, reach + i + 1, size), blocks(0, far, size)]
    for p in range(low_cols // 2):
        cols = blocks(2 * p, 2 * p + 2, size)
        value = part_ref[mine, cols] + jnp.dot(
            left, panel_ref[blocks(0, far, size), cols], preferred_element_type=jnp.float32
        )
        for k in (2 * p, 2 * p + 1):
            block = value[:, blocks(k - 2 * p, k - 2 * p + 1, size)]
            square[:, blocks(k, k + 1, size)] = keep_block(mask_ref, i, k, width, block, square.dtype)
    for p in range(far_cols // 2):
        cols = blocks(2 * p, 2 * p + 2, size)
        low = max(0, 2 * p - reach)
        value = cube_ref[mine, cols] + jnp.dot(
            square[:, blocks(low, low_cols, size)],
            panel_ref[blocks(low, low_cols, size), cols],
            preferred_element_type=jnp.float32,
        )
        if 2 * p < low_cols:
            kept = square[:, cols]
        else:
            kept = high_ref[mine, blocks(2 * p - low_cols, 2 * p + 2 - low_cols, size)]
        result[:, cols] = (3.0 * kept.astype(jnp.float32) - 2.0 * value).astype(result.dtype)
    scalars.wait()
    for s in range(2 * half):
        place = pl.multiple_of(own_place(columns_ref, i + reach, s, far_cols) * size, size)
        target = stay_ref if s < half else leave_ref
        target[0, s % half] = result[:, pl.ds(place, size)]


def write_rows(pieces, out_ref, sems):
    straight = lax.axis_index("col") == 0
    copies = []
    for rows_ref, here, there in pieces:
        for n in range(rows_ref.shape[0]):
            to = out_ref.at[jnp.where(straight, here, there) + n]
            copies.append(pltpu.make_async_copy(rows_ref.at[n], to, sems.at[len(copies)]))
    for copy in copies:
        copy.start()
    for copy in copies:
        copy.wait()


def store_kernel(*refs):
    *row_refs, out_ref, sems = refs
    rows = out_ref.shape[0]
    far = sum(ref.shape[0] == 1 for ref in row_refs) // 2 + 1
    kept, near_ref, got_near_ref, got = row_refs[:far], row_refs[far], row_refs[far + 1], row_refs[far + 2 :]
    near = near_ref.shape[0]
    pieces = [(ref, i, rows - 1 - i) for i, ref in enumerate(kept)]
    pieces.append((near_ref, far, rows - far - near))
    pieces.append((got_near_ref, rows - far - near, far))
    pieces += [(ref, rows - 2 - i, 1 + i) for i, ref in enumerate(got)]
    write_rows(pieces, out_ref, sems)


def finish_kernel(got_ref, before_ref, out_ref, sems):
    write_rows(((got_ref, out_ref.shape[0] - got_ref.shape[0], 0),), out_ref, sems)


def local(matrix, columns):
    local_rows, own_slots, size = matrix.shape[:3]
    dtype = matrix.dtype
    reach = REACH
    far = reach // 2
    near = reach - far
    cols = lax.axis_size("col")
    ring = lax.axis_size("row")
    width = local_rows + reach
    low_cols = reach + far
    far_cols = 2 * reach + far
    same = [(r * cols, (r + 1) % ring * cols) for r in range(ring)] + [
        (r * cols + 1, (r - 1) % ring * cols + 1) for r in range(ring)
    ]
    swap = [(r * cols + 1, (r + 1) % ring * cols) for r in range(ring)] + [
        (r * cols, (r - 1) % ring * cols + 1) for r in range(ring)
    ]
    beside = [(i, (i + 1) % cols) for i in range(cols)]
    axes = ("row", "col")
    edge_rows = own_slots * size
    in_place = pltpu.with_memory_space_constraint(matrix, pltpu.HBM)
    same_edge, swap_edge, held = pl.pallas_call(
        functools.partial(edge_kernel, HEAD),
        out_shape=(
            jax.ShapeDtypeStruct((edge_rows + TILE, size), dtype),
            jax.ShapeDtypeStruct((edge_rows, size), dtype),
            jax.ShapeDtypeStruct(columns.shape, columns.dtype),
        ),
        in_specs=[HBM, HBM],
        out_specs=(VMEM,) * 3,
        scratch_shapes=[pltpu.VMEM((TILE, size), jnp.float32), pltpu.SemaphoreType.DMA((3,))],
        compiler_params=limit(1),
        cost_estimate=LIGHT,
        name="edge",
    )(pltpu.with_memory_space_constraint(columns, pltpu.HBM), in_place)
    same_rows = lax.ppermute(same_edge, axes, same)
    swap_rows = lax.ppermute(swap_edge, axes, swap)
    sent, held = lax.optimization_barrier((matrix, held))
    other = lax.ppermute(sent, "col", beside)

    lead = reach - HEAD
    scalars = pltpu.SMEM(columns.shape, columns.dtype)
    panel_shape = jax.ShapeDtypeStruct((width * size, (width + 1) * size), dtype)
    first_shape = jax.ShapeDtypeStruct((reach * size, width * size), jnp.float32)
    base_shapes = (panel_shape, first_shape, jax.ShapeDtypeStruct((reach * width, size), jnp.float32))

    def base(turn, *before):
        return pl.pallas_call(
            functools.partial(base_kernel, turn),
            out_shape=base_shapes,
            in_specs=[VMEM, HBM, VMEM] + [VMEM] * len(before),
            out_specs=(VMEM,) * 3,
            input_output_aliases={3 + n: n for n in range(len(before))},
            scratch_shapes=[
                pltpu.VMEM(matrix.shape, dtype),
                scalars,
                pltpu.SMEM((reach, width + 1), jnp.int32),
                pltpu.SemaphoreType.DMA((2,)),
            ],
            compiler_params=limit(12),
            cost_estimate=LIGHT,
            name="base",
        )(held, in_place, other, *before)

    early = base(0)
    packed = pl.pallas_call(
        pack_kernel,
        out_shape=tuple(
            jax.ShapeDtypeStruct((reach + 1 + f, size, size), dtype) for f in range(lead)
        ),
        in_specs=[VMEM, HBM, VMEM, ANY],
        out_specs=(VMEM,) * lead,
        scratch_shapes=[
            pltpu.VMEM((lead,) + matrix.shape[1:], dtype),
            scalars,
            pltpu.SemaphoreType.DMA((2,)),
        ],
        compiler_params=limit(2),
        cost_estimate=LIGHT,
        name="pack",
    )(held, in_place, other, early[2])
    arrived = {f: lax.ppermute(packed[f], axes, swap) for f in reversed(range(lead))}

    panel, first_part, mask = base(1, *early)
    panel, first_part = pl.pallas_call(
        functools.partial(lead_kernel, own_slots),
        out_shape=(panel_shape, first_shape),
        in_specs=[VMEM] * 4,
        out_specs=(VMEM,) * 2,
        input_output_aliases={2: 0, 3: 1},
        scratch_shapes=[
            pltpu.VMEM((TILE, size), jnp.int32),
            pltpu.SMEM((TILE, size), jnp.int32),
            pltpu.SemaphoreType.DMA,
        ],
        compiler_params=limit(12),
        cost_estimate=MEDIUM,
        name="lead",
    )(same_rows, swap_rows, panel, first_part)

    rows_out = jax.ShapeDtypeStruct((near, own_slots, size, size), dtype)
    panel, stay_near, leave_near, part, high, cube = pl.pallas_call(
        functools.partial(near_kernel, far),
        out_shape=(
            panel_shape,
            rows_out,
            rows_out,
            jax.ShapeDtypeStruct((far * size, low_cols * size), jnp.float32),
            jax.ShapeDtypeStruct((far * size, (far_cols - low_cols) * size), dtype),
            jax.ShapeDtypeStruct((far * size, far_cols * size), jnp.float32),
        ),
        in_specs=[VMEM] * (4 + lead - far),
        out_specs=(VMEM,) * 6,
        input_output_aliases={3: 0},
        scratch_shapes=[
            pltpu.VMEM((reach * size, width * size), dtype),
            pltpu.VMEM((near * size, (width + 1) * size), dtype),
            scalars,
            pltpu.SemaphoreType.DMA,
        ],
        compiler_params=limit(16),
        cost_estimate=SHORT,
        name="near",
    )(held, mask, first_part, panel, *[arrived[f] for f in range(far, lead)])
    arrived_near = lax.ppermute(leave_near, "col", beside)

    row_out = jax.ShapeDtypeStruct((1, own_slots, size, size), dtype)
    stay, got = {}, {}
    for i in reversed(range(far)):
        panel, stay[i], leave = pl.pallas_call(
            functools.partial(far_kernel, far, i),
            out_shape=(panel_shape, row_out, row_out),
            in_specs=[VMEM] * 7,
            out_specs=(VMEM,) * 3,
            input_output_aliases={6: 0},
            scratch_shapes=[
                pltpu.VMEM((size, low_cols * size), dtype),
                pltpu.VMEM((size, (far_cols + 1) * size), dtype),
                scalars,
                pltpu.SemaphoreType.DMA,
            ],
            compiler_params=limit(16),
            cost_estimate=HEAVY if i else LIGHT,
            name="far",
        )(held, mask, part, high, cube, arrived[i], panel)
        got[i] = lax.ppermute(leave, "col", beside)
    pieces = [*[stay[i] for i in range(far)], stay_near, arrived_near, *[got[i] for i in range(1, far)]]
    out = pl.pallas_call(
        store_kernel,
        out_shape=jax.ShapeDtypeStruct(matrix.shape, dtype),
        in_specs=[VMEM] * len(pieces),
        out_specs=HBM,
        scratch_shapes=[pltpu.SemaphoreType.DMA((local_rows - 1,))],
        compiler_params=limit(1),
        cost_estimate=LIGHT,
        name="store",
    )(*pieces)
    return pl.pallas_call(
        finish_kernel,
        out_shape=jax.ShapeDtypeStruct(matrix.shape, dtype),
        in_specs=[VMEM, HBM],
        out_specs=HBM,
        input_output_aliases={1: 0},
        scratch_shapes=[pltpu.SemaphoreType.DMA((1,))],
        compiler_params=limit(1),
        cost_estimate=LIGHT,
        name="finish",
    )(got[0], out)


def solution(mesh):
    placed = (P(("geom", "row"), "col", None, None), P("row", None))
    return jax.shard_map(
        local,
        mesh=mesh,
        in_specs=placed,
        out_specs=P(("geom", "row"), "col", None, None),
        check_vma=False,
    )
```

```python
import functools

import jax
import jax.numpy as jnp
from jax import lax
from jax.experimental import pallas as pl
from jax.experimental.pallas import tpu as pltpu
from jax.sharding import PartitionSpec as P

REACH = 4
HEAD = 1
MIB = 1024 * 1024
ABSENT = 64
TILE = 16

HEAVY = pl.CostEstimate(flops=20_000_000_000, bytes_accessed=0, transcendentals=0)
LIGHT = pl.CostEstimate(flops=0, bytes_accessed=0, transcendentals=0)
SHORT = pl.CostEstimate(flops=500_000_000, bytes_accessed=0, transcendentals=0)
MEDIUM = pl.CostEstimate(flops=1_200_000_000, bytes_accessed=0, transcendentals=0)

SMEM = pl.BlockSpec(memory_space=pltpu.SMEM)
VMEM = pl.BlockSpec(memory_space=pltpu.VMEM)
ANY = pl.BlockSpec(memory_space=pl.ANY)
HBM = pl.BlockSpec(memory_space=pltpu.HBM)


def limit(mib):
    return pltpu.CompilerParams(vmem_limit_bytes=mib * MIB)


def blocks(first, last, size):
    return slice(first * size, last * size)


def own_place(columns_ref, q, s, limit):
    rows, slots = columns_ref.shape
    flip = lax.axis_index("col")
    row = jnp.where(flip == 0, q - REACH, rows + REACH - 1 - q)
    slot = lax.rem(s + flip * (slots // 2), slots)
    total = rows * lax.axis_size("row")
    column = columns_ref[row, slot]
    step = column - lax.axis_index("row") * rows - row
    step = jnp.where(step > REACH, step - total, step)
    step = jnp.where(step < -REACH, step + total, step)
    place = jnp.where(flip == 0, q + step, q - step)
    inside = (column >= 0) & (place >= 0) & (place < limit)
    return jnp.where(inside, place, limit)


def halo_place(steps_ref, rows, slots, q, s, limit):
    flip = lax.axis_index("col")
    row = jnp.where(flip == 0, rows - REACH + q, REACH - 1 - q)
    slot = lax.rem(s + flip * (slots // 2), slots)
    step = steps_ref[row, slot]
    place = jnp.where(flip == 0, q + step, q - step)
    inside = (step <= REACH) & (place >= 0) & (place < limit)
    return jnp.where(inside, place, limit)


def edge_kernel(near, columns_ref, matrix_ref, *refs):
    rows, half, size = matrix_ref.shape[:3]
    same_refs, swap_refs = refs[:near], refs[near : 2 * near]
    copied_ref, steps, sems = refs[2 * near :]
    straight = lax.axis_index("col") == 0
    copies = []
    for n in range(near):
        up, down = rows - 1 - n, n
        for s in range(half):
            at = blocks(s, s + 1, size)
            source = matrix_ref.at[jnp.where(straight, up, down), s]
            copies.append(pltpu.make_async_copy(source, same_refs[n].at[at], sems.at[0]))
            source = matrix_ref.at[jnp.where(straight, down, up), s]
            copies.append(pltpu.make_async_copy(source, swap_refs[n].at[at], sems.at[1]))
    held = pltpu.make_async_copy(columns_ref, copied_ref, sems.at[2])
    held.start()
    for copy in copies:
        copy.start()
    held.wait()
    column = copied_ref[...]
    row = lax.broadcasted_iota(jnp.int32, column.shape, 0) + lax.axis_index("row") * rows
    total = rows * lax.axis_size("row")
    step = column - row
    step = jnp.where(step > REACH, step - total, step)
    step = jnp.where(step < -REACH, step + total, step)
    step = jnp.where(column >= 0, step, ABSENT)
    steps[...] = jnp.zeros_like(steps)
    steps[:rows, : column.shape[1]] = step.astype(jnp.float32)
    same_refs[0][half * size :, :] = steps[...].astype(same_refs[0].dtype)
    for copy in copies:
        copy.wait()


def pack_kernel(held_ref, matrix_ref, other_ref, after_ref, *refs):
    out_refs, (own, columns_ref, sems) = refs[:-3], refs[-3:]
    rows, half = other_ref.shape[:2]
    lead = own.shape[0]
    straight = lax.axis_index("col") == 0
    start = jnp.where(straight, REACH - lead, rows - REACH)
    copies = [
        pltpu.make_async_copy(held_ref, columns_ref, sems.at[0]),
        pltpu.make_async_copy(matrix_ref.at[pl.ds(start, lead)], own, sems.at[1]),
    ]
    for copy in copies:
        copy.start()
    for out_ref in out_refs:
        out_ref[...] = jnp.zeros_like(out_ref)
    for copy in copies:
        copy.wait()
    for f, out_ref in enumerate(out_refs):
        q = 2 * REACH - 1 - f
        index = jnp.where(straight, lead - 1 - f, f)
        count = REACH + 1 + f
        for s in range(2 * half):
            place = 2 * REACH - 1 - own_place(columns_ref, q, s, 2 * REACH + 1)

            @pl.when((place >= 0) & (place < count))
            def _(place=place, index=index, s=s, out_ref=out_ref):
                if s < half:
                    out_ref[place] = own[index, s]
                else:
                    out_ref[place] = other_ref[start + index, s - half]


def base_kernel(turn, held_ref, matrix_ref, other_ref, *refs):
    panel_ref, first_ref, mask_ref, spot_ref, own_ref, columns_ref, keep_ref, sems = refs[-8:]
    rows, half, size = own_ref.shape[0], own_ref.shape[1], own_ref.shape[2]
    reach = REACH
    width = rows + reach

    @pl.when(lax.rem(lax.axis_index("row") + lax.axis_index("col"), 2) == turn)
    def _():
        copies = [
            pltpu.make_async_copy(held_ref, columns_ref, sems.at[0]),
            pltpu.make_async_copy(matrix_ref, own_ref, sems.at[1]),
        ]
        for copy in copies:
            copy.start()
        panel_ref[...] = jnp.zeros_like(panel_ref)
        for copy in copies:
            copy.wait()
        for q in range(reach, width):
            index = jnp.where(lax.axis_index("col") == 0, q - reach, width - 1 - q)
            for s in range(2 * half):
                place = pl.multiple_of(own_place(columns_ref, q, s, width) * size, size)
                source = own_ref if s < half else other_ref
                panel_ref[blocks(q, q + 1, size), pl.ds(place, size)] = source[index, s % half]
        for i in range(reach):
            for k in range(width + 1):
                keep_ref[i, k] = 0
            for s in range(2 * half):
                keep_ref[i, own_place(columns_ref, i + reach, s, width)] = 1
            for k in range(width):
                at = i * width + k
                mask_ref[at : at + 1, :] = jnp.full((1, size), keep_ref[i, k], jnp.float32)
        window = 2 * reach + 1
        for i in range(spot_ref.shape[0] // (2 * half * window)):
            for s in range(2 * half):
                place = own_place(columns_ref, i + reach, s, width)
                for d in range(window):
                    at = (i * 2 * half + s) * window + d
                    taken = jnp.where(place == i + d, 1, 0)
                    spot_ref[at : at + 1, :] = jnp.full((1, size), taken, jnp.float32)
        for p in range(width // 2):
            low = max(reach, 2 * p - reach)
            high = min(width, 2 * p + 2 + reach)
            cols = blocks(2 * p, 2 * p + 2, size)
            first_ref[:, cols] = jnp.dot(
                panel_ref[blocks(reach, 2 * reach, size), blocks(low, high, size)],
                panel_ref[blocks(low, high, size), cols],
                preferred_element_type=jnp.float32,
            )


def lead_kernel(
    half, same_ref, swap_ref, before_panel, before_first, panel_ref, first_ref, steps, halo_ref, sem
):
    size = same_ref.shape[1]
    reach = REACH
    width = panel_ref.shape[0] // size
    lead = reach - HEAD
    steps[...] = same_ref[half * size :, :].astype(jnp.float32).astype(jnp.int32)
    copy = pltpu.make_async_copy(steps, halo_ref, sem)
    copy.start()
    copy.wait()
    for s in range(2 * half):
        place = halo_place(halo_ref, width - reach, 2 * half, lead, s, width)
        place = pl.multiple_of(place * size, size)
        source = same_ref if s < half else swap_ref
        panel_ref[blocks(lead, lead + 1, size), pl.ds(place, size)] = source[
            blocks(s % half, s % half + 1, size), :
        ]
    left = panel_ref[blocks(reach, 2 * reach, size), blocks(lead, reach, size)]
    for p in range(reach):
        cols = blocks(2 * p, 2 * p + 2, size)
        first_ref[:, cols] += jnp.dot(
            left, panel_ref[blocks(lead, reach, size), cols], preferred_element_type=jnp.float32
        )


def keep_block(mask_ref, i, k, width, block, dtype):
    if abs(i + REACH - k) > REACH:
        return jnp.zeros(block.shape, dtype)
    return jnp.where(mask_ref[i * width + k : i * width + k + 1, :] > 0, block, 0.0).astype(dtype)


def near_kernel(
    far, held_ref, mask_ref, first_ref, before_ref, *refs
):
    mid_refs = refs[: REACH - HEAD - far]
    (
        panel_ref, stay_ref, leave_ref, part_ref, high_ref, cube_ref, square, result, columns_ref, sem,
    ) = refs[REACH - HEAD - far :]
    reach = REACH
    lead = reach - HEAD
    scalars = pltpu.make_async_copy(held_ref, columns_ref, sem)
    scalars.start()
    half, size = stay_ref.shape[1], stay_ref.shape[2]
    width = panel_ref.shape[0] // size
    near = reach - far
    low_cols = reach + far
    far_cols = 2 * reach + far
    near_cols = 2 * reach
    for q, mid_ref in zip(range(far, lead), mid_refs):
        for k in range(reach + 1 + q):
            panel_ref[blocks(q, q + 1, size), blocks(k, k + 1, size)] = mid_ref[k]
    result[:, blocks(width, width + 1, size)] = jnp.zeros((near * size, size), result.dtype)
    left = panel_ref[blocks(reach, 2 * reach, size), blocks(far, lead, size)]
    for p in range(width // 2):
        cols = blocks(2 * p, 2 * p + 2, size)
        value = first_ref[:, cols]
        if 2 * p < near_cols:
            value = value + jnp.dot(
                left, panel_ref[blocks(far, lead, size), cols], preferred_element_type=jnp.float32
            )
        for i in range(reach):
            for k in (2 * p, 2 * p + 1):
                block = value[blocks(i, i + 1, size), blocks(k - 2 * p, k - 2 * p + 1, size)]
                here = (blocks(i, i + 1, size), blocks(k, k + 1, size))
                if i < far and k < low_cols:
                    part_ref[here] = block
                    square[here] = jnp.zeros((size, size), square.dtype)
                else:
                    square[here] = keep_block(mask_ref, i, k, width, block, square.dtype)
    rest = slice(far * size, reach * size)
    for p in range(width // 2):
        cols = blocks(2 * p, 2 * p + 2, size)
        low = max(far, 2 * p - reach)
        high = min(width, 2 * p + 2 + reach)
        value = jnp.dot(
            square[rest, blocks(low, high, size)],
            panel_ref[blocks(low, high, size), cols],
            preferred_element_type=jnp.float32,
        )
        result[:, cols] = (3.0 * square[rest, cols].astype(jnp.float32) - 2.0 * value).astype(result.dtype)
        low = max(low_cols, 2 * p - reach)
        high = min(far_cols, 2 * p + 2 + reach)
        if 2 * p < far_cols:
            if low < high:
                cube_ref[:, cols] = jnp.dot(
                    square[: far * size, blocks(low, high, size)],
                    panel_ref[blocks(low, high, size), cols],
                    preferred_element_type=jnp.float32,
                )
            else:
                cube_ref[:, cols] = jnp.zeros((far * size, 2 * size), jnp.float32)
    high_ref[...] = square[: far * size, blocks(low_cols, far_cols, size)]
    scalars.wait()
    for i in range(near):
        index = jnp.where(lax.axis_index("col") == 0, i, near - 1 - i)
        for s in range(2 * half):
            place = pl.multiple_of(own_place(columns_ref, i + reach + far, s, width) * size, size)
            target = stay_ref if s < half else leave_ref
            target[index, s % half] = result[blocks(i, i + 1, size), pl.ds(place, size)]


def far_kernel(
    far, i, mask_ref, spot_ref, part_ref, high_ref, cube_ref, row_ref, before_ref,
    panel_ref, stay_ref, leave_ref, square, result
):
    reach = REACH
    half, size = stay_ref.shape[1], stay_ref.shape[2]
    width = panel_ref.shape[0] // size
    low_cols = reach + far
    far_cols = 2 * reach + far
    mine = blocks(i, i + 1, size)
    for k in range(reach + 1 + i):
        panel_ref[mine, blocks(k, k + 1, size)] = row_ref[k]
    left = panel_ref[blocks(reach + i, reach + i + 1, size), blocks(0, far, size)]
    for p in range(low_cols // 2):
        cols = blocks(2 * p, 2 * p + 2, size)
        value = part_ref[mine, cols] + jnp.dot(
            left, panel_ref[blocks(0, far, size), cols], preferred_element_type=jnp.float32
        )
        for k in (2 * p, 2 * p + 1):
            block = value[:, blocks(k - 2 * p, k - 2 * p + 1, size)]
            square[:, blocks(k, k + 1, size)] = keep_block(mask_ref, i, k, width, block, square.dtype)
    for p in range(far_cols // 2):
        cols = blocks(2 * p, 2 * p + 2, size)
        low = max(0, 2 * p - reach)
        value = cube_ref[mine, cols] + jnp.dot(
            square[:, blocks(low, low_cols, size)],
            panel_ref[blocks(low, low_cols, size), cols],
            preferred_element_type=jnp.float32,
        )
        if 2 * p < low_cols:
            kept = square[:, cols]
        else:
            kept = high_ref[mine, blocks(2 * p - low_cols, 2 * p + 2 - low_cols, size)]
        result[:, cols] = (3.0 * kept.astype(jnp.float32) - 2.0 * value).astype(result.dtype)
    window = 2 * reach + 1
    for s in range(2 * half):
        block = jnp.zeros((size, size), result.dtype)
        for d in range(window):
            at = (i * 2 * half + s) * window + d
            block = jnp.where(spot_ref[at : at + 1, :] > 0, result[:, blocks(i + d, i + d + 1, size)], block)
        target = stay_ref if s < half else leave_ref
        target[0, s % half] = block


def write_rows(pieces, out_ref, sems):
    straight = lax.axis_index("col") == 0
    copies = []
    for rows_ref, here, there in pieces:
        for n in range(rows_ref.shape[0]):
            to = out_ref.at[jnp.where(straight, here, there) + n]
            copies.append(pltpu.make_async_copy(rows_ref.at[n], to, sems.at[len(copies)]))
    for copy in copies:
        copy.start()
    for copy in copies:
        copy.wait()


def store_kernel(*refs):
    *row_refs, out_ref, sems = refs
    rows = out_ref.shape[0]
    far = sum(ref.shape[0] == 1 for ref in row_refs) // 2 + 1
    kept, near_ref, got_near_ref, got = row_refs[:far], row_refs[far], row_refs[far + 1], row_refs[far + 2 :]
    near = near_ref.shape[0]
    pieces = [(ref, i, rows - 1 - i) for i, ref in enumerate(kept)]
    pieces.append((near_ref, far, rows - far - near))
    pieces.append((got_near_ref, rows - far - near, far))
    pieces += [(ref, rows - 2 - i, 1 + i) for i, ref in enumerate(got)]
    write_rows(pieces, out_ref, sems)


def finish_kernel(got_ref, before_ref, out_ref, sems):
    write_rows(((got_ref, out_ref.shape[0] - got_ref.shape[0], 0),), out_ref, sems)


def local(matrix, columns):
    local_rows, own_slots, size = matrix.shape[:3]
    dtype = matrix.dtype
    reach = REACH
    far = reach // 2
    near = reach - far
    cols = lax.axis_size("col")
    ring = lax.axis_size("row")
    width = local_rows + reach
    low_cols = reach + far
    far_cols = 2 * reach + far
    same = [(r * cols, (r + 1) % ring * cols) for r in range(ring)] + [
        (r * cols + 1, (r - 1) % ring * cols + 1) for r in range(ring)
    ]
    swap = [(r * cols + 1, (r + 1) % ring * cols) for r in range(ring)] + [
        (r * cols, (r - 1) % ring * cols + 1) for r in range(ring)
    ]
    beside = [(i, (i + 1) % cols) for i in range(cols)]
    axes = ("row", "col")
    edge_rows = own_slots * size
    in_place = pltpu.with_memory_space_constraint(matrix, pltpu.HBM)
    same_edge, swap_edge, held = pl.pallas_call(
        functools.partial(edge_kernel, HEAD),
        out_shape=(
            jax.ShapeDtypeStruct((edge_rows + TILE, size), dtype),
            jax.ShapeDtypeStruct((edge_rows, size), dtype),
            jax.ShapeDtypeStruct(columns.shape, columns.dtype),
        ),
        in_specs=[HBM, HBM],
        out_specs=(VMEM,) * 3,
        scratch_shapes=[pltpu.VMEM((TILE, size), jnp.float32), pltpu.SemaphoreType.DMA((3,))],
        compiler_params=limit(1),
        cost_estimate=LIGHT,
        name="edge",
    )(pltpu.with_memory_space_constraint(columns, pltpu.HBM), in_place)
    same_rows = lax.ppermute(same_edge, axes, same)
    swap_rows = lax.ppermute(swap_edge, axes, swap)
    sent, held = lax.optimization_barrier((matrix, held))
    other = lax.ppermute(sent, "col", beside)

    lead = reach - HEAD
    scalars = pltpu.SMEM(columns.shape, columns.dtype)
    panel_shape = jax.ShapeDtypeStruct((width * size, (width + 1) * size), dtype)
    first_shape = jax.ShapeDtypeStruct((reach * size, width * size), jnp.float32)
    base_shapes = (
        panel_shape,
        first_shape,
        jax.ShapeDtypeStruct((reach * width, size), jnp.float32),
        jax.ShapeDtypeStruct((far * 2 * own_slots * (2 * reach + 1), size), jnp.float32),
    )

    def base(turn, *before):
        return pl.pallas_call(
            functools.partial(base_kernel, turn),
            out_shape=base_shapes,
            in_specs=[VMEM, HBM, VMEM] + [VMEM] * len(before),
            out_specs=(VMEM,) * 4,
            input_output_aliases={3 + n: n for n in range(len(before))},
            scratch_shapes=[
                pltpu.VMEM(matrix.shape, dtype),
                scalars,
                pltpu.SMEM((reach, width + 1), jnp.int32),
                pltpu.SemaphoreType.DMA((2,)),
            ],
            compiler_params=limit(12),
            cost_estimate=LIGHT,
            name="base",
        )(held, in_place, other, *before)

    early = base(0)
    packed = pl.pallas_call(
        pack_kernel,
        out_shape=tuple(
            jax.ShapeDtypeStruct((reach + 1 + f, size, size), dtype) for f in range(lead)
        ),
        in_specs=[VMEM, HBM, VMEM, ANY],
        out_specs=(VMEM,) * lead,
        scratch_shapes=[
            pltpu.VMEM((lead,) + matrix.shape[1:], dtype),
            scalars,
            pltpu.SemaphoreType.DMA((2,)),
        ],
        compiler_params=limit(2),
        cost_estimate=LIGHT,
        name="pack",
    )(held, in_place, other, early[2])
    arrived = {f: lax.ppermute(packed[f], axes, swap) for f in reversed(range(lead))}

    panel, first_part, mask, spot = base(1, *early)
    panel, first_part = pl.pallas_call(
        functools.partial(lead_kernel, own_slots),
        out_shape=(panel_shape, first_shape),
        in_specs=[VMEM] * 4,
        out_specs=(VMEM,) * 2,
        input_output_aliases={2: 0, 3: 1},
        scratch_shapes=[
            pltpu.VMEM((TILE, size), jnp.int32),
            pltpu.SMEM((TILE, size), jnp.int32),
            pltpu.SemaphoreType.DMA,
        ],
        compiler_params=limit(12),
        cost_estimate=MEDIUM,
        name="lead",
    )(same_rows, swap_rows, panel, first_part)

    rows_out = jax.ShapeDtypeStruct((near, own_slots, size, size), dtype)
    panel, stay_near, leave_near, part, high, cube = pl.pallas_call(
        functools.partial(near_kernel, far),
        out_shape=(
            panel_shape,
            rows_out,
            rows_out,
            jax.ShapeDtypeStruct((far * size, low_cols * size), jnp.float32),
            jax.ShapeDtypeStruct((far * size, (far_cols - low_cols) * size), dtype),
            jax.ShapeDtypeStruct((far * size, far_cols * size), jnp.float32),
        ),
        in_specs=[VMEM] * (4 + lead - far),
        out_specs=(VMEM,) * 6,
        input_output_aliases={3: 0},
        scratch_shapes=[
            pltpu.VMEM((reach * size, width * size), dtype),
            pltpu.VMEM((near * size, (width + 1) * size), dtype),
            scalars,
            pltpu.SemaphoreType.DMA,
        ],
        compiler_params=limit(16),
        cost_estimate=SHORT,
        name="near",
    )(held, mask, first_part, panel, *[arrived[f] for f in range(far, lead)])
    arrived_near = lax.ppermute(leave_near, "col", beside)

    row_out = jax.ShapeDtypeStruct((1, own_slots, size, size), dtype)
    stay, got = {}, {}
    for i in reversed(range(far)):
        panel, stay[i], leave = pl.pallas_call(
            functools.partial(far_kernel, far, i),
            out_shape=(panel_shape, row_out, row_out),
            in_specs=[VMEM] * 7,
            out_specs=(VMEM,) * 3,
            input_output_aliases={6: 0},
            scratch_shapes=[
                pltpu.VMEM((size, low_cols * size), dtype),
                pltpu.VMEM((size, far_cols * size), dtype),
            ],
            compiler_params=limit(16),
            cost_estimate=HEAVY if i else LIGHT,
            name="far",
        )(mask, spot, part, high, cube, arrived[i], panel)
        got[i] = lax.ppermute(leave, "col", beside)
    pieces = [*[stay[i] for i in range(far)], stay_near, arrived_near, *[got[i] for i in range(1, far)]]
    out = pl.pallas_call(
        store_kernel,
        out_shape=jax.ShapeDtypeStruct(matrix.shape, dtype),
        in_specs=[VMEM] * len(pieces),
        out_specs=HBM,
        scratch_shapes=[pltpu.SemaphoreType.DMA((local_rows - 1,))],
        compiler_params=limit(1),
        cost_estimate=LIGHT,
        name="store",
    )(*pieces)
    return pl.pallas_call(
        finish_kernel,
        out_shape=jax.ShapeDtypeStruct(matrix.shape, dtype),
        in_specs=[VMEM, HBM],
        out_specs=HBM,
        input_output_aliases={1: 0},
        scratch_shapes=[pltpu.SemaphoreType.DMA((1,))],
        compiler_params=limit(1),
        cost_estimate=LIGHT,
        name="finish",
    )(got[0], out)


def solution(mesh):
    placed = (P(("geom", "row"), "col", None, None), P("row", None))
    return jax.shard_map(
        local,
        mesh=mesh,
        in_specs=placed,
        out_specs=P(("geom", "row"), "col", None, None),
        check_vma=False,
    )
```

```python
import functools

import jax
import jax.numpy as jnp
from jax import lax
from jax.experimental import pallas as pl
from jax.experimental.pallas import tpu as pltpu
from jax.sharding import PartitionSpec as P

REACH = 4
HEAD = 1
MIB = 1024 * 1024
ABSENT = 64
TILE = 16

HEAVY = pl.CostEstimate(flops=20_000_000_000, bytes_accessed=0, transcendentals=0)
LIGHT = pl.CostEstimate(flops=0, bytes_accessed=0, transcendentals=0)
SHORT = pl.CostEstimate(flops=500_000_000, bytes_accessed=0, transcendentals=0)
MEDIUM = pl.CostEstimate(flops=1_200_000_000, bytes_accessed=0, transcendentals=0)

SMEM = pl.BlockSpec(memory_space=pltpu.SMEM)
VMEM = pl.BlockSpec(memory_space=pltpu.VMEM)
ANY = pl.BlockSpec(memory_space=pl.ANY)
HBM = pl.BlockSpec(memory_space=pltpu.HBM)


def limit(mib):
    return pltpu.CompilerParams(vmem_limit_bytes=mib * MIB)


def blocks(first, last, size):
    return slice(first * size, last * size)


def own_place(columns_ref, q, s, limit):
    rows, slots = columns_ref.shape
    flip = lax.axis_index("col")
    row = jnp.where(flip == 0, q - REACH, rows + REACH - 1 - q)
    slot = lax.rem(s + flip * (slots // 2), slots)
    total = rows * lax.axis_size("row")
    column = columns_ref[row, slot]
    step = column - lax.axis_index("row") * rows - row
    step = jnp.where(step > REACH, step - total, step)
    step = jnp.where(step < -REACH, step + total, step)
    place = jnp.where(flip == 0, q + step, q - step)
    inside = (column >= 0) & (place >= 0) & (place < limit)
    return jnp.where(inside, place, limit)


def halo_place(steps_ref, rows, slots, q, s, limit):
    flip = lax.axis_index("col")
    row = jnp.where(flip == 0, rows - REACH + q, REACH - 1 - q)
    slot = lax.rem(s + flip * (slots // 2), slots)
    step = steps_ref[row, slot]
    place = jnp.where(flip == 0, q + step, q - step)
    inside = (step <= REACH) & (place >= 0) & (place < limit)
    return jnp.where(inside, place, limit)


def edge_kernel(near, columns_ref, matrix_ref, *refs):
    rows, half, size = matrix_ref.shape[:3]
    same_refs, swap_refs = refs[:near], refs[near : 2 * near]
    copied_ref, steps, sems = refs[2 * near :]
    straight = lax.axis_index("col") == 0
    copies = []
    for n in range(near):
        up, down = rows - 1 - n, n
        for s in range(half):
            at = blocks(s, s + 1, size)
            source = matrix_ref.at[jnp.where(straight, up, down), s]
            copies.append(pltpu.make_async_copy(source, same_refs[n].at[at], sems.at[0]))
            source = matrix_ref.at[jnp.where(straight, down, up), s]
            copies.append(pltpu.make_async_copy(source, swap_refs[n].at[at], sems.at[1]))
    held = pltpu.make_async_copy(columns_ref, copied_ref, sems.at[2])
    held.start()
    for copy in copies:
        copy.start()
    held.wait()
    column = copied_ref[...]
    row = lax.broadcasted_iota(jnp.int32, column.shape, 0) + lax.axis_index("row") * rows
    total = rows * lax.axis_size("row")
    step = column - row
    step = jnp.where(step > REACH, step - total, step)
    step = jnp.where(step < -REACH, step + total, step)
    step = jnp.where(column >= 0, step, ABSENT)
    steps[...] = jnp.zeros_like(steps)
    steps[:rows, : column.shape[1]] = step.astype(jnp.float32)
    same_refs[0][half * size :, :] = steps[...].astype(same_refs[0].dtype)
    for copy in copies:
        copy.wait()


def pack_kernel(held_ref, matrix_ref, other_ref, *refs):
    out_refs, (own, columns_ref, sems) = refs[:-3], refs[-3:]
    rows, half = other_ref.shape[:2]
    lead = own.shape[0]
    straight = lax.axis_index("col") == 0
    start = jnp.where(straight, REACH - lead, rows - REACH)
    copies = [
        pltpu.make_async_copy(held_ref, columns_ref, sems.at[0]),
        pltpu.make_async_copy(matrix_ref.at[pl.ds(start, lead)], own, sems.at[1]),
    ]
    for copy in copies:
        copy.start()
    for out_ref in out_refs:
        out_ref[...] = jnp.zeros_like(out_ref)
    for copy in copies:
        copy.wait()
    for f, out_ref in enumerate(out_refs):
        q = 2 * REACH - 1 - f
        index = jnp.where(straight, lead - 1 - f, f)
        count = REACH + 1 + f
        for s in range(2 * half):
            place = 2 * REACH - 1 - own_place(columns_ref, q, s, 2 * REACH + 1)

            @pl.when((place >= 0) & (place < count))
            def _(place=place, index=index, s=s, out_ref=out_ref):
                if s < half:
                    out_ref[place] = own[index, s]
                else:
                    out_ref[place] = other_ref[start + index, s - half]


def base_kernel(
    held_ref, matrix_ref, other_ref,
    panel_ref, first_ref, mask_ref, spot_ref, own_ref, columns_ref, keep_ref, sems
):
    rows, half, size = own_ref.shape[0], own_ref.shape[1], own_ref.shape[2]
    reach = REACH
    width = rows + reach

    copies = [
        pltpu.make_async_copy(held_ref, columns_ref, sems.at[0]),
        pltpu.make_async_copy(matrix_ref, own_ref, sems.at[1]),
    ]
    for copy in copies:
        copy.start()
    panel_ref[...] = jnp.zeros_like(panel_ref)
    for copy in copies:
        copy.wait()
    for q in range(reach, width):
        index = jnp.where(lax.axis_index("col") == 0, q - reach, width - 1 - q)
        for s in range(2 * half):
            place = pl.multiple_of(own_place(columns_ref, q, s, width) * size, size)
            source = own_ref if s < half else other_ref
            panel_ref[blocks(q, q + 1, size), pl.ds(place, size)] = source[index, s % half]
    for i in range(reach):
        for k in range(width + 1):
            keep_ref[i, k] = 0
        for s in range(2 * half):
            keep_ref[i, own_place(columns_ref, i + reach, s, width)] = 1
        for k in range(width):
            at = i * width + k
            mask_ref[at : at + 1, :] = jnp.full((1, size), keep_ref[i, k], jnp.float32)
    window = 2 * reach + 1
    for i in range(spot_ref.shape[0] // (2 * half * window)):
        for s in range(2 * half):
            place = own_place(columns_ref, i + reach, s, width)
            for d in range(window):
                at = (i * 2 * half + s) * window + d
                taken = jnp.where(place == i + d, 1, 0)
                spot_ref[at : at + 1, :] = jnp.full((1, size), taken, jnp.float32)
    for p in range(width // 2):
        low = max(reach, 2 * p - reach)
        high = min(width, 2 * p + 2 + reach)
        cols = blocks(2 * p, 2 * p + 2, size)
        first_ref[:, cols] = jnp.dot(
            panel_ref[blocks(reach, 2 * reach, size), blocks(low, high, size)],
            panel_ref[blocks(low, high, size), cols],
            preferred_element_type=jnp.float32,
        )


def lead_kernel(
    half, same_ref, swap_ref, before_panel, before_first, panel_ref, first_ref, steps, halo_ref, sem
):
    size = same_ref.shape[1]
    reach = REACH
    width = panel_ref.shape[0] // size
    lead = reach - HEAD
    steps[...] = same_ref[half * size :, :].astype(jnp.float32).astype(jnp.int32)
    copy = pltpu.make_async_copy(steps, halo_ref, sem)
    copy.start()
    copy.wait()
    for s in range(2 * half):
        place = halo_place(halo_ref, width - reach, 2 * half, lead, s, width)
        place = pl.multiple_of(place * size, size)
        source = same_ref if s < half else swap_ref
        panel_ref[blocks(lead, lead + 1, size), pl.ds(place, size)] = source[
            blocks(s % half, s % half + 1, size), :
        ]
    left = panel_ref[blocks(reach, 2 * reach, size), blocks(lead, reach, size)]
    for p in range(reach):
        cols = blocks(2 * p, 2 * p + 2, size)
        first_ref[:, cols] += jnp.dot(
            left, panel_ref[blocks(lead, reach, size), cols], preferred_element_type=jnp.float32
        )


def keep_block(mask_ref, i, k, width, block, dtype):
    if abs(i + REACH - k) > REACH:
        return jnp.zeros(block.shape, dtype)
    return jnp.where(mask_ref[i * width + k : i * width + k + 1, :] > 0, block, 0.0).astype(dtype)


def near_kernel(
    far, held_ref, mask_ref, first_ref, before_ref, *refs
):
    mid_refs = refs[: REACH - HEAD - far]
    (
        panel_ref, stay_ref, leave_ref, part_ref, high_ref, cube_ref, square, result, columns_ref, sem,
    ) = refs[REACH - HEAD - far :]
    reach = REACH
    lead = reach - HEAD
    scalars = pltpu.make_async_copy(held_ref, columns_ref, sem)
    scalars.start()
    half, size = stay_ref.shape[1], stay_ref.shape[2]
    width = panel_ref.shape[0] // size
    near = reach - far
    low_cols = reach + far
    far_cols = 2 * reach + far
    near_cols = 2 * reach
    for q, mid_ref in zip(range(far, lead), mid_refs):
        for k in range(reach + 1 + q):
            panel_ref[blocks(q, q + 1, size), blocks(k, k + 1, size)] = mid_ref[k]
    result[:, blocks(width, width + 1, size)] = jnp.zeros((near * size, size), result.dtype)
    left = panel_ref[blocks(reach, 2 * reach, size), blocks(far, lead, size)]
    for p in range(width // 2):
        cols = blocks(2 * p, 2 * p + 2, size)
        value = first_ref[:, cols]
        if 2 * p < near_cols:
            value = value + jnp.dot(
                left, panel_ref[blocks(far, lead, size), cols], preferred_element_type=jnp.float32
            )
        for i in range(reach):
            for k in (2 * p, 2 * p + 1):
                block = value[blocks(i, i + 1, size), blocks(k - 2 * p, k - 2 * p + 1, size)]
                here = (blocks(i, i + 1, size), blocks(k, k + 1, size))
                if i < far and k < low_cols:
                    part_ref[here] = block
                    square[here] = jnp.zeros((size, size), square.dtype)
                else:
                    square[here] = keep_block(mask_ref, i, k, width, block, square.dtype)
    rest = slice(far * size, reach * size)
    for p in range(width // 2):
        cols = blocks(2 * p, 2 * p + 2, size)
        low = max(far, 2 * p - reach)
        high = min(width, 2 * p + 2 + reach)
        value = jnp.dot(
            square[rest, blocks(low, high, size)],
            panel_ref[blocks(low, high, size), cols],
            preferred_element_type=jnp.float32,
        )
        result[:, cols] = (3.0 * square[rest, cols].astype(jnp.float32) - 2.0 * value).astype(result.dtype)
        low = max(low_cols, 2 * p - reach)
        high = min(far_cols, 2 * p + 2 + reach)
        if 2 * p < far_cols:
            if low < high:
                cube_ref[:, cols] = jnp.dot(
                    square[: far * size, blocks(low, high, size)],
                    panel_ref[blocks(low, high, size), cols],
                    preferred_element_type=jnp.float32,
                )
            else:
                cube_ref[:, cols] = jnp.zeros((far * size, 2 * size), jnp.float32)
    high_ref[...] = square[: far * size, blocks(low_cols, far_cols, size)]
    scalars.wait()
    for i in range(near):
        index = jnp.where(lax.axis_index("col") == 0, i, near - 1 - i)
        for s in range(2 * half):
            place = pl.multiple_of(own_place(columns_ref, i + reach + far, s, width) * size, size)
            target = stay_ref if s < half else leave_ref
            target[index, s % half] = result[blocks(i, i + 1, size), pl.ds(place, size)]


def far_kernel(
    far, i, mask_ref, spot_ref, part_ref, high_ref, cube_ref, row_ref, before_ref,
    panel_ref, stay_ref, leave_ref, square, result
):
    reach = REACH
    half, size = stay_ref.shape[1], stay_ref.shape[2]
    width = panel_ref.shape[0] // size
    low_cols = reach + far
    far_cols = 2 * reach + far
    mine = blocks(i, i + 1, size)
    for k in range(reach + 1 + i):
        panel_ref[mine, blocks(k, k + 1, size)] = row_ref[k]
    left = panel_ref[blocks(reach + i, reach + i + 1, size), blocks(0, far, size)]
    for p in range(low_cols // 2):
        cols = blocks(2 * p, 2 * p + 2, size)
        value = part_ref[mine, cols] + jnp.dot(
            left, panel_ref[blocks(0, far, size), cols], preferred_element_type=jnp.float32
        )
        for k in (2 * p, 2 * p + 1):
            block = value[:, blocks(k - 2 * p, k - 2 * p + 1, size)]
            square[:, blocks(k, k + 1, size)] = keep_block(mask_ref, i, k, width, block, square.dtype)
    for p in range(far_cols // 2):
        cols = blocks(2 * p, 2 * p + 2, size)
        low = max(0, 2 * p - reach)
        value = cube_ref[mine, cols] + jnp.dot(
            square[:, blocks(low, low_cols, size)],
            panel_ref[blocks(low, low_cols, size), cols],
            preferred_element_type=jnp.float32,
        )
        if 2 * p < low_cols:
            kept = square[:, cols]
        else:
            kept = high_ref[mine, blocks(2 * p - low_cols, 2 * p + 2 - low_cols, size)]
        result[:, cols] = (3.0 * kept.astype(jnp.float32) - 2.0 * value).astype(result.dtype)
    window = 2 * reach + 1
    for s in range(2 * half):
        block = jnp.zeros((size, size), result.dtype)
        for d in range(window):
            at = (i * 2 * half + s) * window + d
            block = jnp.where(spot_ref[at : at + 1, :] > 0, result[:, blocks(i + d, i + d + 1, size)], block)
        target = stay_ref if s < half else leave_ref
        target[0, s % half] = block


def write_rows(pieces, out_ref, sems):
    straight = lax.axis_index("col") == 0
    copies = []
    for rows_ref, here, there in pieces:
        for n in range(rows_ref.shape[0]):
            to = out_ref.at[jnp.where(straight, here, there) + n]
            copies.append(pltpu.make_async_copy(rows_ref.at[n], to, sems.at[len(copies)]))
    for copy in copies:
        copy.start()
    for copy in copies:
        copy.wait()


def store_kernel(*refs):
    *row_refs, out_ref, sems = refs
    rows = out_ref.shape[0]
    far = sum(ref.shape[0] == 1 for ref in row_refs) // 2 + 1
    kept, near_ref, got_near_ref, got = row_refs[:far], row_refs[far], row_refs[far + 1], row_refs[far + 2 :]
    near = near_ref.shape[0]
    pieces = [(ref, i, rows - 1 - i) for i, ref in enumerate(kept)]
    pieces.append((near_ref, far, rows - far - near))
    pieces.append((got_near_ref, rows - far - near, far))
    pieces += [(ref, rows - 2 - i, 1 + i) for i, ref in enumerate(got)]
    write_rows(pieces, out_ref, sems)


def finish_kernel(got_ref, before_ref, out_ref, sems):
    write_rows(((got_ref, out_ref.shape[0] - got_ref.shape[0], 0),), out_ref, sems)


def local(matrix, columns):
    local_rows, own_slots, size = matrix.shape[:3]
    dtype = matrix.dtype
    reach = REACH
    far = reach // 2
    near = reach - far
    cols = lax.axis_size("col")
    ring = lax.axis_size("row")
    width = local_rows + reach
    low_cols = reach + far
    far_cols = 2 * reach + far
    same = [(r * cols, (r + 1) % ring * cols) for r in range(ring)] + [
        (r * cols + 1, (r - 1) % ring * cols + 1) for r in range(ring)
    ]
    swap = [(r * cols + 1, (r + 1) % ring * cols) for r in range(ring)] + [
        (r * cols, (r - 1) % ring * cols + 1) for r in range(ring)
    ]
    beside = [(i, (i + 1) % cols) for i in range(cols)]
    axes = ("row", "col")
    edge_rows = own_slots * size
    in_place = pltpu.with_memory_space_constraint(matrix, pltpu.HBM)
    same_edge, swap_edge, held = pl.pallas_call(
        functools.partial(edge_kernel, HEAD),
        out_shape=(
            jax.ShapeDtypeStruct((edge_rows + TILE, size), dtype),
            jax.ShapeDtypeStruct((edge_rows, size), dtype),
            jax.ShapeDtypeStruct(columns.shape, columns.dtype),
        ),
        in_specs=[HBM, HBM],
        out_specs=(VMEM,) * 3,
        scratch_shapes=[pltpu.VMEM((TILE, size), jnp.float32), pltpu.SemaphoreType.DMA((3,))],
        compiler_params=limit(1),
        cost_estimate=LIGHT,
        name="edge",
    )(pltpu.with_memory_space_constraint(columns, pltpu.HBM), in_place)
    same_rows = lax.ppermute(same_edge, axes, same)
    swap_rows = lax.ppermute(swap_edge, axes, swap)
    sent, held = lax.optimization_barrier((matrix, held))
    other = lax.ppermute(sent, "col", beside)

    lead = reach - HEAD
    scalars = pltpu.SMEM(columns.shape, columns.dtype)
    panel_shape = jax.ShapeDtypeStruct((width * size, (width + 1) * size), dtype)
    first_shape = jax.ShapeDtypeStruct((reach * size, width * size), jnp.float32)
    base_shapes = (
        panel_shape,
        first_shape,
        jax.ShapeDtypeStruct((reach * width, size), jnp.float32),
        jax.ShapeDtypeStruct((far * 2 * own_slots * (2 * reach + 1), size), jnp.float32),
    )

    packed = pl.pallas_call(
        pack_kernel,
        out_shape=tuple(
            jax.ShapeDtypeStruct((reach + 1 + f, size, size), dtype) for f in range(lead)
        ),
        in_specs=[VMEM, HBM, VMEM],
        out_specs=(VMEM,) * lead,
        scratch_shapes=[
            pltpu.VMEM((lead,) + matrix.shape[1:], dtype),
            scalars,
            pltpu.SemaphoreType.DMA((2,)),
        ],
        compiler_params=limit(2),
        cost_estimate=LIGHT,
        name="pack",
    )(held, in_place, other)
    arrived = {f: lax.ppermute(packed[f], axes, swap) for f in reversed(range(lead))}

    panel, first_part, mask, spot = pl.pallas_call(
        base_kernel,
        out_shape=base_shapes,
        in_specs=[VMEM, HBM, VMEM],
        out_specs=(VMEM,) * 4,
        scratch_shapes=[
            pltpu.VMEM(matrix.shape, dtype),
            scalars,
            pltpu.SMEM((reach, width + 1), jnp.int32),
            pltpu.SemaphoreType.DMA((2,)),
        ],
        compiler_params=limit(12),
        cost_estimate=LIGHT,
        name="base",
    )(held, in_place, other)
    panel, first_part = pl.pallas_call(
        functools.partial(lead_kernel, own_slots),
        out_shape=(panel_shape, first_shape),
        in_specs=[VMEM] * 4,
        out_specs=(VMEM,) * 2,
        input_output_aliases={2: 0, 3: 1},
        scratch_shapes=[
            pltpu.VMEM((TILE, size), jnp.int32),
            pltpu.SMEM((TILE, size), jnp.int32),
            pltpu.SemaphoreType.DMA,
        ],
        compiler_params=limit(12),
        cost_estimate=MEDIUM,
        name="lead",
    )(same_rows, swap_rows, panel, first_part)

    rows_out = jax.ShapeDtypeStruct((near, own_slots, size, size), dtype)
    panel, stay_near, leave_near, part, high, cube = pl.pallas_call(
        functools.partial(near_kernel, far),
        out_shape=(
            panel_shape,
            rows_out,
            rows_out,
            jax.ShapeDtypeStruct((far * size, low_cols * size), jnp.float32),
            jax.ShapeDtypeStruct((far * size, (far_cols - low_cols) * size), dtype),
            jax.ShapeDtypeStruct((far * size, far_cols * size), jnp.float32),
        ),
        in_specs=[VMEM] * (4 + lead - far),
        out_specs=(VMEM,) * 6,
        input_output_aliases={3: 0},
        scratch_shapes=[
            pltpu.VMEM((reach * size, width * size), dtype),
            pltpu.VMEM((near * size, (width + 1) * size), dtype),
            scalars,
            pltpu.SemaphoreType.DMA,
        ],
        compiler_params=limit(16),
        cost_estimate=SHORT,
        name="near",
    )(held, mask, first_part, panel, *[arrived[f] for f in range(far, lead)])
    arrived_near = lax.ppermute(leave_near, "col", beside)

    row_out = jax.ShapeDtypeStruct((1, own_slots, size, size), dtype)
    stay, got = {}, {}
    for i in reversed(range(far)):
        panel, stay[i], leave = pl.pallas_call(
            functools.partial(far_kernel, far, i),
            out_shape=(panel_shape, row_out, row_out),
            in_specs=[VMEM] * 7,
            out_specs=(VMEM,) * 3,
            input_output_aliases={6: 0},
            scratch_shapes=[
                pltpu.VMEM((size, low_cols * size), dtype),
                pltpu.VMEM((size, far_cols * size), dtype),
            ],
            compiler_params=limit(16),
            cost_estimate=HEAVY if i else LIGHT,
            name="far",
        )(mask, spot, part, high, cube, arrived[i], panel)
        got[i] = lax.ppermute(leave, "col", beside)
    pieces = [*[stay[i] for i in range(far)], stay_near, arrived_near, *[got[i] for i in range(1, far)]]
    out = pl.pallas_call(
        store_kernel,
        out_shape=jax.ShapeDtypeStruct(matrix.shape, dtype),
        in_specs=[VMEM] * len(pieces),
        out_specs=HBM,
        scratch_shapes=[pltpu.SemaphoreType.DMA((local_rows - 1,))],
        compiler_params=limit(1),
        cost_estimate=LIGHT,
        name="store",
    )(*pieces)
    return pl.pallas_call(
        finish_kernel,
        out_shape=jax.ShapeDtypeStruct(matrix.shape, dtype),
        in_specs=[VMEM, HBM],
        out_specs=HBM,
        input_output_aliases={1: 0},
        scratch_shapes=[pltpu.SemaphoreType.DMA((1,))],
        compiler_params=limit(1),
        cost_estimate=LIGHT,
        name="finish",
    )(got[0], out)


def solution(mesh):
    placed = (P(("geom", "row"), "col", None, None), P("row", None))
    return jax.shard_map(
        local,
        mesh=mesh,
        in_specs=placed,
        out_specs=P(("geom", "row"), "col", None, None),
        check_vma=False,
    )
```

```python
import functools

import jax
import jax.numpy as jnp
from jax import lax
from jax.experimental import pallas as pl
from jax.experimental.pallas import tpu as pltpu
from jax.sharding import PartitionSpec as P

REACH = 4
HEAD = 1
MIB = 1024 * 1024
ABSENT = 64
TILE = 16

HEAVY = pl.CostEstimate(flops=20_000_000_000, bytes_accessed=0, transcendentals=0)
LIGHT = pl.CostEstimate(flops=0, bytes_accessed=0, transcendentals=0)
SHORT = pl.CostEstimate(flops=500_000_000, bytes_accessed=0, transcendentals=0)
MEDIUM = pl.CostEstimate(flops=1_200_000_000, bytes_accessed=0, transcendentals=0)

SMEM = pl.BlockSpec(memory_space=pltpu.SMEM)
VMEM = pl.BlockSpec(memory_space=pltpu.VMEM)
ANY = pl.BlockSpec(memory_space=pl.ANY)
HBM = pl.BlockSpec(memory_space=pltpu.HBM)


def limit(mib):
    return pltpu.CompilerParams(vmem_limit_bytes=mib * MIB)


def blocks(first, last, size):
    return slice(first * size, last * size)


def own_place(columns_ref, q, s, limit):
    rows, slots = columns_ref.shape
    flip = lax.axis_index("col")
    row = jnp.where(flip == 0, q - REACH, rows + REACH - 1 - q)
    slot = lax.rem(s + flip * (slots // 2), slots)
    total = rows * lax.axis_size("row")
    column = columns_ref[row, slot]
    step = column - lax.axis_index("row") * rows - row
    step = jnp.where(step > REACH, step - total, step)
    step = jnp.where(step < -REACH, step + total, step)
    place = jnp.where(flip == 0, q + step, q - step)
    inside = (column >= 0) & (place >= 0) & (place < limit)
    return jnp.where(inside, place, limit)


def halo_place(steps_ref, rows, slots, q, s, limit):
    flip = lax.axis_index("col")
    row = jnp.where(flip == 0, rows - REACH + q, REACH - 1 - q)
    slot = lax.rem(s + flip * (slots // 2), slots)
    step = steps_ref[row, slot]
    place = jnp.where(flip == 0, q + step, q - step)
    inside = (step <= REACH) & (place >= 0) & (place < limit)
    return jnp.where(inside, place, limit)


def edge_kernel(near, columns_ref, matrix_ref, *refs):
    rows, half, size = matrix_ref.shape[:3]
    same_refs, swap_refs = refs[:near], refs[near : 2 * near]
    copied_ref, steps, sems = refs[2 * near :]
    straight = lax.axis_index("col") == 0
    copies = []
    for n in range(near):
        up, down = rows - 1 - n, n
        for s in range(half):
            at = blocks(s, s + 1, size)
            source = matrix_ref.at[jnp.where(straight, up, down), s]
            copies.append(pltpu.make_async_copy(source, same_refs[n].at[at], sems.at[0]))
            source = matrix_ref.at[jnp.where(straight, down, up), s]
            copies.append(pltpu.make_async_copy(source, swap_refs[n].at[at], sems.at[1]))
    held = pltpu.make_async_copy(columns_ref, copied_ref, sems.at[2])
    held.start()
    for copy in copies:
        copy.start()
    held.wait()
    column = copied_ref[...]
    row = lax.broadcasted_iota(jnp.int32, column.shape, 0) + lax.axis_index("row") * rows
    total = rows * lax.axis_size("row")
    step = column - row
    step = jnp.where(step > REACH, step - total, step)
    step = jnp.where(step < -REACH, step + total, step)
    step = jnp.where(column >= 0, step, ABSENT)
    steps[...] = jnp.zeros_like(steps)
    steps[:rows, : column.shape[1]] = step.astype(jnp.float32)
    same_refs[0][half * size :, :] = steps[...].astype(same_refs[0].dtype)
    for copy in copies:
        copy.wait()


def pack_kernel(held_ref, matrix_ref, other_ref, after_ref, *refs):
    out_refs, (own, columns_ref, sems) = refs[:-3], refs[-3:]
    rows, half = other_ref.shape[:2]
    lead = own.shape[0]
    straight = lax.axis_index("col") == 0
    start = jnp.where(straight, REACH - lead, rows - REACH)
    copies = [
        pltpu.make_async_copy(held_ref, columns_ref, sems.at[0]),
        pltpu.make_async_copy(matrix_ref.at[pl.ds(start, lead)], own, sems.at[1]),
    ]
    for copy in copies:
        copy.start()
    for out_ref in out_refs:
        out_ref[...] = jnp.zeros_like(out_ref)
    for copy in copies:
        copy.wait()
    for f, out_ref in enumerate(out_refs):
        q = 2 * REACH - 1 - f
        index = jnp.where(straight, lead - 1 - f, f)
        count = REACH + 1 + f
        for s in range(2 * half):
            place = 2 * REACH - 1 - own_place(columns_ref, q, s, 2 * REACH + 1)

            @pl.when((place >= 0) & (place < count))
            def _(place=place, index=index, s=s, out_ref=out_ref):
                if s < half:
                    out_ref[place] = own[index, s]
                else:
                    out_ref[place] = other_ref[start + index, s - half]


def base_kernel(turn, held_ref, matrix_ref, other_ref, *refs):
    panel_ref, first_ref, mask_ref, spot_ref, own_ref, columns_ref, keep_ref, sems = refs[-8:]
    rows, half, size = own_ref.shape[0], own_ref.shape[1], own_ref.shape[2]
    reach = REACH
    width = rows + reach

    @pl.when(lax.rem(lax.axis_index("row") + lax.axis_index("col"), 2) == turn)
    def _():
        copies = [
            pltpu.make_async_copy(held_ref, columns_ref, sems.at[0]),
            pltpu.make_async_copy(matrix_ref, own_ref, sems.at[1]),
        ]
        for copy in copies:
            copy.start()
        panel_ref[...] = jnp.zeros_like(panel_ref)
        for copy in copies:
            copy.wait()
        for q in range(reach, width):
            index = jnp.where(lax.axis_index("col") == 0, q - reach, width - 1 - q)
            for s in range(2 * half):
                place = pl.multiple_of(own_place(columns_ref, q, s, width) * size, size)
                source = own_ref if s < half else other_ref
                panel_ref[blocks(q, q + 1, size), pl.ds(place, size)] = source[index, s % half]
        for i in range(reach):
            for k in range(width + 1):
                keep_ref[i, k] = 0
            for s in range(2 * half):
                keep_ref[i, own_place(columns_ref, i + reach, s, width)] = 1
            for k in range(width):
                at = i * width + k
                mask_ref[at : at + 1, :] = jnp.full((1, size), keep_ref[i, k], jnp.float32)
        window = 2 * reach + 1
        for i in range(spot_ref.shape[0] // (2 * half * window)):
            for s in range(2 * half):
                place = own_place(columns_ref, i + reach, s, width)
                for d in range(window):
                    at = (i * 2 * half + s) * window + d
                    taken = jnp.where(place == i + d, 1, 0)
                    spot_ref[at : at + 1, :] = jnp.full((1, size), taken, jnp.float32)
        for p in range(width // 2):
            low = max(reach, 2 * p - reach)
            high = min(width, 2 * p + 2 + reach)
            cols = blocks(2 * p, 2 * p + 2, size)
            first_ref[:, cols] = jnp.dot(
                panel_ref[blocks(reach, 2 * reach, size), blocks(low, high, size)],
                panel_ref[blocks(low, high, size), cols],
                preferred_element_type=jnp.float32,
            )


def lead_kernel(
    half, same_ref, swap_ref, before_panel, before_first, panel_ref, first_ref, steps, halo_ref, sem
):
    size = same_ref.shape[1]
    reach = REACH
    width = panel_ref.shape[0] // size
    lead = reach - HEAD
    steps[...] = same_ref[half * size :, :].astype(jnp.float32).astype(jnp.int32)
    copy = pltpu.make_async_copy(steps, halo_ref, sem)
    copy.start()
    copy.wait()
    for s in range(2 * half):
        place = halo_place(halo_ref, width - reach, 2 * half, lead, s, width)
        place = pl.multiple_of(place * size, size)
        source = same_ref if s < half else swap_ref
        panel_ref[blocks(lead, lead + 1, size), pl.ds(place, size)] = source[
            blocks(s % half, s % half + 1, size), :
        ]
    left = panel_ref[blocks(reach, 2 * reach, size), blocks(lead, reach, size)]
    for p in range(reach):
        cols = blocks(2 * p, 2 * p + 2, size)
        first_ref[:, cols] += jnp.dot(
            left, panel_ref[blocks(lead, reach, size), cols], preferred_element_type=jnp.float32
        )


def keep_block(mask_ref, i, k, width, block, dtype):
    if abs(i + REACH - k) > REACH:
        return jnp.zeros(block.shape, dtype)
    return jnp.where(mask_ref[i * width + k : i * width + k + 1, :] > 0, block, 0.0).astype(dtype)


def near_kernel(
    far, held_ref, mask_ref, first_ref, before_ref, *refs
):
    mid_refs = refs[: REACH - HEAD - far]
    (
        panel_ref, stay_ref, leave_ref, part_ref, high_ref, cube_ref, square, result, columns_ref, sem,
    ) = refs[REACH - HEAD - far :]
    reach = REACH
    lead = reach - HEAD
    scalars = pltpu.make_async_copy(held_ref, columns_ref, sem)
    scalars.start()
    half, size = stay_ref.shape[1], stay_ref.shape[2]
    width = panel_ref.shape[0] // size
    near = reach - far
    low_cols = reach + far
    far_cols = 2 * reach + far
    near_cols = 2 * reach
    for q, mid_ref in zip(range(far, lead), mid_refs):
        for k in range(reach + 1 + q):
            panel_ref[blocks(q, q + 1, size), blocks(k, k + 1, size)] = mid_ref[k]
    result[:, blocks(width, width + 1, size)] = jnp.zeros((near * size, size), result.dtype)
    left = panel_ref[blocks(reach, 2 * reach, size), blocks(far, lead, size)]
    for p in range(width // 2):
        cols = blocks(2 * p, 2 * p + 2, size)
        value = first_ref[:, cols]
        if 2 * p < near_cols:
            value = value + jnp.dot(
                left, panel_ref[blocks(far, lead, size), cols], preferred_element_type=jnp.float32
            )
        for i in range(reach):
            for k in (2 * p, 2 * p + 1):
                block = value[blocks(i, i + 1, size), blocks(k - 2 * p, k - 2 * p + 1, size)]
                here = (blocks(i, i + 1, size), blocks(k, k + 1, size))
                if i < far and k < low_cols:
                    part_ref[here] = block
                    square[here] = jnp.zeros((size, size), square.dtype)
                else:
                    square[here] = keep_block(mask_ref, i, k, width, block, square.dtype)
    rest = slice(far * size, reach * size)
    for p in range(width // 2):
        cols = blocks(2 * p, 2 * p + 2, size)
        low = max(far, 2 * p - reach)
        high = min(width, 2 * p + 2 + reach)
        value = jnp.dot(
            square[rest, blocks(low, high, size)],
            panel_ref[blocks(low, high, size), cols],
            preferred_element_type=jnp.float32,
        )
        result[:, cols] = (3.0 * square[rest, cols].astype(jnp.float32) - 2.0 * value).astype(result.dtype)
        low = max(low_cols, 2 * p - reach)
        high = min(far_cols, 2 * p + 2 + reach)
        if 2 * p < far_cols:
            if low < high:
                cube_ref[:, cols] = jnp.dot(
                    square[: far * size, blocks(low, high, size)],
                    panel_ref[blocks(low, high, size), cols],
                    preferred_element_type=jnp.float32,
                )
            else:
                cube_ref[:, cols] = jnp.zeros((far * size, 2 * size), jnp.float32)
    high_ref[...] = square[: far * size, blocks(low_cols, far_cols, size)]
    scalars.wait()
    for i in range(near):
        index = jnp.where(lax.axis_index("col") == 0, i, near - 1 - i)
        for s in range(2 * half):
            place = pl.multiple_of(own_place(columns_ref, i + reach + far, s, width) * size, size)
            target = stay_ref if s < half else leave_ref
            target[index, s % half] = result[blocks(i, i + 1, size), pl.ds(place, size)]


def far_kernel(
    far, i, mask_ref, spot_ref, part_ref, high_ref, cube_ref, row_ref, after_ref, before_ref,
    panel_ref, stay_ref, leave_ref, square, scratch
):
    reach = REACH
    result = scratch if i else stay_ref
    half, size = leave_ref.shape[1], leave_ref.shape[2]
    width = panel_ref.shape[0] // size
    low_cols = reach + far
    far_cols = 2 * reach + far
    mine = blocks(i, i + 1, size)
    for k in range(reach + 1 + i):
        panel_ref[mine, blocks(k, k + 1, size)] = row_ref[k]
    left = panel_ref[blocks(reach + i, reach + i + 1, size), blocks(0, far, size)]
    for p in range(low_cols // 2):
        cols = blocks(2 * p, 2 * p + 2, size)
        value = part_ref[mine, cols] + jnp.dot(
            left, panel_ref[blocks(0, far, size), cols], preferred_element_type=jnp.float32
        )
        for k in (2 * p, 2 * p + 1):
            block = value[:, blocks(k - 2 * p, k - 2 * p + 1, size)]
            square[:, blocks(k, k + 1, size)] = keep_block(mask_ref, i, k, width, block, square.dtype)
    for p in range(far_cols // 2):
        cols = blocks(2 * p, 2 * p + 2, size)
        low = max(0, 2 * p - reach)
        value = cube_ref[mine, cols] + jnp.dot(
            square[:, blocks(low, low_cols, size)],
            panel_ref[blocks(low, low_cols, size), cols],
            preferred_element_type=jnp.float32,
        )
        if 2 * p < low_cols:
            kept = square[:, cols]
        else:
            kept = high_ref[mine, blocks(2 * p - low_cols, 2 * p + 2 - low_cols, size)]
        result[:, cols] = (3.0 * kept.astype(jnp.float32) - 2.0 * value).astype(result.dtype)
    for s in range(0 if i else half, 2 * half):
        target = stay_ref if s < half else leave_ref
        target[0, s % half] = chosen(result, spot_ref, i, s, 2 * half)


def chosen(result, spot_ref, i, s, slots):
    size = result.shape[0]
    window = 2 * REACH + 1
    block = jnp.zeros((size, size), result.dtype)
    for d in range(window):
        at = (i * slots + s) * window + d
        block = jnp.where(spot_ref[at : at + 1, :] > 0, result[:, blocks(i + d, i + d + 1, size)], block)
    return block


def start_rows(pieces, out_ref, sems, first=0):
    straight = lax.axis_index("col") == 0
    copies = []
    for rows_ref, here, there in pieces:
        for n in range(rows_ref.shape[0]):
            to = out_ref.at[jnp.where(straight, here, there) + n]
            copies.append(pltpu.make_async_copy(rows_ref.at[n], to, sems.at[first + len(copies)]))
    for copy in copies:
        copy.start()
    return copies


def write_rows(pieces, out_ref, sems):
    for copy in start_rows(pieces, out_ref, sems):
        copy.wait()


def store_near_kernel(near_ref, out_ref, mark_ref, sems):
    rows, near = out_ref.shape[0], near_ref.shape[0]
    write_rows(((near_ref, rows // 2 - near, rows // 2),), out_ref, sems)
    mark_ref[...] = jnp.zeros_like(mark_ref)


def store_kernel(result_ref, spot_ref, got_near_ref, *refs):
    *row_refs, before_ref, out_ref, stay, sems = refs
    rows, near, half = out_ref.shape[0], got_near_ref.shape[0], out_ref.shape[1]
    count = len(row_refs) // 2
    pieces = [(got_near_ref, rows - 1 - count - near, 1 + count)]
    pieces += [(ref, 1 + i, rows - 2 - i) for i, ref in enumerate(row_refs[:count])]
    pieces += [(ref, rows - 2 - i, 1 + i) for i, ref in enumerate(row_refs[count:])]
    copies = start_rows(pieces, out_ref, sems)
    for s in range(half):
        stay[0, s] = chosen(result_ref, spot_ref, 0, s, 2 * half)
    copies += start_rows(((stay, 0, rows - 1),), out_ref, sems, len(copies))
    for copy in copies:
        copy.wait()


def finish_kernel(got_ref, before_ref, out_ref, sems):
    write_rows(((got_ref, out_ref.shape[0] - got_ref.shape[0], 0),), out_ref, sems)


def local(matrix, columns):
    local_rows, own_slots, size = matrix.shape[:3]
    dtype = matrix.dtype
    reach = REACH
    far = reach // 2
    near = reach - far
    cols = lax.axis_size("col")
    ring = lax.axis_size("row")
    width = local_rows + reach
    low_cols = reach + far
    far_cols = 2 * reach + far
    same = [(r * cols, (r + 1) % ring * cols) for r in range(ring)] + [
        (r * cols + 1, (r - 1) % ring * cols + 1) for r in range(ring)
    ]
    swap = [(r * cols + 1, (r + 1) % ring * cols) for r in range(ring)] + [
        (r * cols, (r - 1) % ring * cols + 1) for r in range(ring)
    ]
    beside = [(i, (i + 1) % cols) for i in range(cols)]
    axes = ("row", "col")
    edge_rows = own_slots * size
    in_place = pltpu.with_memory_space_constraint(matrix, pltpu.HBM)
    same_edge, swap_edge, held = pl.pallas_call(
        functools.partial(edge_kernel, HEAD),
        out_shape=(
            jax.ShapeDtypeStruct((edge_rows + TILE, size), dtype),
            jax.ShapeDtypeStruct((edge_rows, size), dtype),
            jax.ShapeDtypeStruct(columns.shape, columns.dtype),
        ),
        in_specs=[HBM, HBM],
        out_specs=(VMEM,) * 3,
        scratch_shapes=[pltpu.VMEM((TILE, size), jnp.float32), pltpu.SemaphoreType.DMA((3,))],
        compiler_params=limit(1),
        cost_estimate=LIGHT,
        name="edge",
    )(pltpu.with_memory_space_constraint(columns, pltpu.HBM), in_place)
    same_rows = lax.ppermute(same_edge, axes, same)
    swap_rows = lax.ppermute(swap_edge, axes, swap)
    sent, held = lax.optimization_barrier((matrix, held))
    other = lax.ppermute(sent, "col", beside)

    lead = reach - HEAD
    scalars = pltpu.SMEM(columns.shape, columns.dtype)
    panel_shape = jax.ShapeDtypeStruct((width * size, (width + 1) * size), dtype)
    first_shape = jax.ShapeDtypeStruct((reach * size, width * size), jnp.float32)
    base_shapes = (
        panel_shape,
        first_shape,
        jax.ShapeDtypeStruct((reach * width, size), jnp.float32),
        jax.ShapeDtypeStruct((far * 2 * own_slots * (2 * reach + 1), size), jnp.float32),
    )

    def base(turn, *before):
        return pl.pallas_call(
            functools.partial(base_kernel, turn),
            out_shape=base_shapes,
            in_specs=[VMEM, HBM, VMEM] + [VMEM] * len(before),
            out_specs=(VMEM,) * 4,
            input_output_aliases={3 + n: n for n in range(len(before))},
            scratch_shapes=[
                pltpu.VMEM(matrix.shape, dtype),
                scalars,
                pltpu.SMEM((reach, width + 1), jnp.int32),
                pltpu.SemaphoreType.DMA((2,)),
            ],
            compiler_params=limit(12),
            cost_estimate=LIGHT,
            name="base",
        )(held, in_place, other, *before)

    early = base(0)
    packed = pl.pallas_call(
        pack_kernel,
        out_shape=tuple(
            jax.ShapeDtypeStruct((reach + 1 + f, size, size), dtype) for f in range(lead)
        ),
        in_specs=[VMEM, HBM, VMEM, ANY],
        out_specs=(VMEM,) * lead,
        scratch_shapes=[
            pltpu.VMEM((lead,) + matrix.shape[1:], dtype),
            scalars,
            pltpu.SemaphoreType.DMA((2,)),
        ],
        compiler_params=limit(2),
        cost_estimate=LIGHT,
        name="pack",
    )(held, in_place, other, early[2])
    arrived = {f: lax.ppermute(packed[f], axes, swap) for f in reversed(range(lead))}

    panel, first_part, mask, spot = base(1, *early)
    panel, first_part = pl.pallas_call(
        functools.partial(lead_kernel, own_slots),
        out_shape=(panel_shape, first_shape),
        in_specs=[VMEM] * 4,
        out_specs=(VMEM,) * 2,
        input_output_aliases={2: 0, 3: 1},
        scratch_shapes=[
            pltpu.VMEM((TILE, size), jnp.int32),
            pltpu.SMEM((TILE, size), jnp.int32),
            pltpu.SemaphoreType.DMA,
        ],
        compiler_params=limit(12),
        cost_estimate=MEDIUM,
        name="lead",
    )(same_rows, swap_rows, panel, first_part)

    rows_out = jax.ShapeDtypeStruct((near, own_slots, size, size), dtype)
    panel, stay_near, leave_near, part, high, cube = pl.pallas_call(
        functools.partial(near_kernel, far),
        out_shape=(
            panel_shape,
            rows_out,
            rows_out,
            jax.ShapeDtypeStruct((far * size, low_cols * size), jnp.float32),
            jax.ShapeDtypeStruct((far * size, (far_cols - low_cols) * size), dtype),
            jax.ShapeDtypeStruct((far * size, far_cols * size), jnp.float32),
        ),
        in_specs=[VMEM] * (4 + lead - far),
        out_specs=(VMEM,) * 6,
        input_output_aliases={3: 0},
        scratch_shapes=[
            pltpu.VMEM((reach * size, width * size), dtype),
            pltpu.VMEM((near * size, (width + 1) * size), dtype),
            scalars,
            pltpu.SemaphoreType.DMA,
        ],
        compiler_params=limit(16),
        cost_estimate=SHORT,
        name="near",
    )(held, mask, first_part, panel, *[arrived[f] for f in range(far, lead)])
    arrived_near = lax.ppermute(leave_near, "col", beside)

    out, mark = pl.pallas_call(
        store_near_kernel,
        out_shape=(jax.ShapeDtypeStruct(matrix.shape, dtype), jax.ShapeDtypeStruct((8, size), jnp.float32)),
        in_specs=[VMEM],
        out_specs=(HBM, VMEM),
        scratch_shapes=[pltpu.SemaphoreType.DMA((near,))],
        compiler_params=limit(1),
        cost_estimate=LIGHT,
        name="store_near",
    )(stay_near)
    row_out = jax.ShapeDtypeStruct((1, own_slots, size, size), dtype)
    result_out = jax.ShapeDtypeStruct((size, far_cols * size), dtype)
    stay, got = {}, {}
    for i in reversed(range(far)):
        panel, stay[i], leave = pl.pallas_call(
            functools.partial(far_kernel, far, i),
            out_shape=(panel_shape, row_out if i else result_out, row_out),
            in_specs=[VMEM] * 8,
            out_specs=(VMEM,) * 3,
            input_output_aliases={7: 0},
            scratch_shapes=[
                pltpu.VMEM((size, low_cols * size), dtype),
                pltpu.VMEM((size, far_cols * size), dtype),
            ],
            compiler_params=limit(16),
            cost_estimate=HEAVY if i else LIGHT,
            name="far",
        )(mask, spot, part, high, cube, arrived[i], mark, panel)
        got[i] = lax.ppermute(leave, "col", beside)
    rest = range(1, far)
    pieces = [stay[0], spot, arrived_near, *[stay[i] for i in rest], *[got[i] for i in rest]]
    out = pl.pallas_call(
        store_kernel,
        out_shape=jax.ShapeDtypeStruct(matrix.shape, dtype),
        in_specs=[VMEM] * len(pieces) + [HBM],
        out_specs=HBM,
        input_output_aliases={len(pieces): 0},
        scratch_shapes=[
            pltpu.VMEM((1,) + matrix.shape[1:], dtype),
            pltpu.SemaphoreType.DMA((local_rows - near - 1,)),
        ],
        compiler_params=limit(2),
        cost_estimate=LIGHT,
        name="store",
    )(*pieces, out)
    return pl.pallas_call(
        finish_kernel,
        out_shape=jax.ShapeDtypeStruct(matrix.shape, dtype),
        in_specs=[VMEM, HBM],
        out_specs=HBM,
        input_output_aliases={1: 0},
        scratch_shapes=[pltpu.SemaphoreType.DMA((1,))],
        compiler_params=limit(1),
        cost_estimate=LIGHT,
        name="finish",
    )(got[0], out)


def solution(mesh):
    placed = (P(("geom", "row"), "col", None, None), P("row", None))
    return jax.shard_map(
        local,
        mesh=mesh,
        in_specs=placed,
        out_specs=P(("geom", "row"), "col", None, None),
        check_vma=False,
    )
```

```python
import functools

import jax
import jax.numpy as jnp
from jax import lax
from jax.experimental import pallas as pl
from jax.experimental.pallas import tpu as pltpu
from jax.sharding import PartitionSpec as P

REACH = 4
HEAD = 1
MIB = 1024 * 1024
ABSENT = 64
TILE = 16

HEAVY = pl.CostEstimate(flops=20_000_000_000, bytes_accessed=0, transcendentals=0)
LIGHT = pl.CostEstimate(flops=0, bytes_accessed=0, transcendentals=0)
SHORT = pl.CostEstimate(flops=500_000_000, bytes_accessed=0, transcendentals=0)
MEDIUM = pl.CostEstimate(flops=1_200_000_000, bytes_accessed=0, transcendentals=0)

SMEM = pl.BlockSpec(memory_space=pltpu.SMEM)
VMEM = pl.BlockSpec(memory_space=pltpu.VMEM)
ANY = pl.BlockSpec(memory_space=pl.ANY)
HBM = pl.BlockSpec(memory_space=pltpu.HBM)


def limit(mib):
    return pltpu.CompilerParams(vmem_limit_bytes=mib * MIB)


def blocks(first, last, size):
    return slice(first * size, last * size)


def own_place(columns_ref, q, s, limit):
    rows, slots = columns_ref.shape
    flip = lax.axis_index("col")
    row = jnp.where(flip == 0, q - REACH, rows + REACH - 1 - q)
    slot = lax.rem(s + flip * (slots // 2), slots)
    total = rows * lax.axis_size("row")
    column = columns_ref[row, slot]
    step = column - lax.axis_index("row") * rows - row
    step = jnp.where(step > REACH, step - total, step)
    step = jnp.where(step < -REACH, step + total, step)
    place = jnp.where(flip == 0, q + step, q - step)
    inside = (column >= 0) & (place >= 0) & (place < limit)
    return jnp.where(inside, place, limit)


def halo_place(steps_ref, rows, slots, q, s, limit):
    flip = lax.axis_index("col")
    row = jnp.where(flip == 0, rows - REACH + q, REACH - 1 - q)
    slot = lax.rem(s + flip * (slots // 2), slots)
    step = steps_ref[row, slot]
    place = jnp.where(flip == 0, q + step, q - step)
    inside = (step <= REACH) & (place >= 0) & (place < limit)
    return jnp.where(inside, place, limit)


def edge_kernel(near, columns_ref, matrix_ref, *refs):
    rows, half, size = matrix_ref.shape[:3]
    same_refs, swap_refs = refs[:near], refs[near : 2 * near]
    copied_ref, steps, sems = refs[2 * near :]
    straight = lax.axis_index("col") == 0
    copies = []
    for n in range(near):
        up, down = rows - 1 - n, n
        for s in range(half):
            at = blocks(s, s + 1, size)
            source = matrix_ref.at[jnp.where(straight, up, down), s]
            copies.append(pltpu.make_async_copy(source, same_refs[n].at[at], sems.at[0]))
            source = matrix_ref.at[jnp.where(straight, down, up), s]
            copies.append(pltpu.make_async_copy(source, swap_refs[n].at[at], sems.at[1]))
    held = pltpu.make_async_copy(columns_ref, copied_ref, sems.at[2])
    held.start()
    for copy in copies:
        copy.start()
    held.wait()
    column = copied_ref[...]
    row = lax.broadcasted_iota(jnp.int32, column.shape, 0) + lax.axis_index("row") * rows
    total = rows * lax.axis_size("row")
    step = column - row
    step = jnp.where(step > REACH, step - total, step)
    step = jnp.where(step < -REACH, step + total, step)
    step = jnp.where(column >= 0, step, ABSENT)
    steps[...] = jnp.zeros_like(steps)
    steps[:rows, : column.shape[1]] = step.astype(jnp.float32)
    same_refs[0][half * size :, :] = steps[...].astype(same_refs[0].dtype)
    for copy in copies:
        copy.wait()


def pack_kernel(held_ref, matrix_ref, other_ref, after_ref, *refs):
    out_refs, (own, columns_ref, sems) = refs[:-3], refs[-3:]
    rows, half = other_ref.shape[:2]
    lead = own.shape[0]
    straight = lax.axis_index("col") == 0
    start = jnp.where(straight, REACH - lead, rows - REACH)
    copies = [
        pltpu.make_async_copy(held_ref, columns_ref, sems.at[0]),
        pltpu.make_async_copy(matrix_ref.at[pl.ds(start, lead)], own, sems.at[1]),
    ]
    for copy in copies:
        copy.start()
    for out_ref in out_refs:
        out_ref[...] = jnp.zeros_like(out_ref)
    for copy in copies:
        copy.wait()
    for f, out_ref in enumerate(out_refs):
        q = 2 * REACH - 1 - f
        index = jnp.where(straight, lead - 1 - f, f)
        count = REACH + 1 + f
        for s in range(2 * half):
            place = 2 * REACH - 1 - own_place(columns_ref, q, s, 2 * REACH + 1)

            @pl.when((place >= 0) & (place < count))
            def _(place=place, index=index, s=s, out_ref=out_ref):
                if s < half:
                    out_ref[place] = own[index, s]
                else:
                    out_ref[place] = other_ref[start + index, s - half]


def base_kernel(turn, held_ref, matrix_ref, other_ref, *refs):
    panel_ref, first_ref, mask_ref, spot_ref, own_ref, columns_ref, keep_ref, sems = refs[-8:]
    rows, half, size = own_ref.shape[0], own_ref.shape[1], own_ref.shape[2]
    reach = REACH
    width = rows + reach

    @pl.when(lax.rem(lax.axis_index("row") + lax.axis_index("col"), 2) == turn)
    def _():
        copies = [
            pltpu.make_async_copy(held_ref, columns_ref, sems.at[0]),
            pltpu.make_async_copy(matrix_ref, own_ref, sems.at[1]),
        ]
        for copy in copies:
            copy.start()
        panel_ref[...] = jnp.zeros_like(panel_ref)
        for copy in copies:
            copy.wait()
        for q in range(reach, width):
            index = jnp.where(lax.axis_index("col") == 0, q - reach, width - 1 - q)
            for s in range(2 * half):
                place = pl.multiple_of(own_place(columns_ref, q, s, width) * size, size)
                source = own_ref if s < half else other_ref
                panel_ref[blocks(q, q + 1, size), pl.ds(place, size)] = source[index, s % half]
        for i in range(reach):
            for k in range(width + 1):
                keep_ref[i, k] = 0
            for s in range(2 * half):
                keep_ref[i, own_place(columns_ref, i + reach, s, width)] = 1
            for k in range(width):
                at = i * width + k
                mask_ref[at : at + 1, :] = jnp.full((1, size), keep_ref[i, k], jnp.float32)
        window = 2 * reach + 1
        for i in range(spot_ref.shape[0] // (2 * half * window)):
            for s in range(2 * half):
                place = own_place(columns_ref, i + reach, s, width)
                for d in range(window):
                    at = (i * 2 * half + s) * window + d
                    taken = jnp.where(place == i + d, 1, 0)
                    spot_ref[at : at + 1, :] = jnp.full((1, size), taken, jnp.float32)
        for p in range(width // 2):
            low = max(reach, 2 * p - reach)
            high = min(width, 2 * p + 2 + reach)
            cols = blocks(2 * p, 2 * p + 2, size)
            first_ref[:, cols] = jnp.dot(
                panel_ref[blocks(reach, 2 * reach, size), blocks(low, high, size)],
                panel_ref[blocks(low, high, size), cols],
                preferred_element_type=jnp.float32,
            )


def lead_kernel(
    half, same_ref, swap_ref, before_panel, before_first, panel_ref, first_ref, steps, halo_ref, sem
):
    size = same_ref.shape[1]
    reach = REACH
    width = panel_ref.shape[0] // size
    lead = reach - HEAD
    steps[...] = same_ref[half * size :, :].astype(jnp.float32).astype(jnp.int32)
    copy = pltpu.make_async_copy(steps, halo_ref, sem)
    copy.start()
    copy.wait()
    for s in range(2 * half):
        place = halo_place(halo_ref, width - reach, 2 * half, lead, s, width)
        place = pl.multiple_of(place * size, size)
        source = same_ref if s < half else swap_ref
        panel_ref[blocks(lead, lead + 1, size), pl.ds(place, size)] = source[
            blocks(s % half, s % half + 1, size), :
        ]
    left = panel_ref[blocks(reach, 2 * reach, size), blocks(lead, reach, size)]
    for p in range(reach):
        cols = blocks(2 * p, 2 * p + 2, size)
        first_ref[:, cols] += jnp.dot(
            left, panel_ref[blocks(lead, reach, size), cols], preferred_element_type=jnp.float32
        )


def keep_block(mask_ref, i, k, width, block, dtype):
    if abs(i + REACH - k) > REACH:
        return jnp.zeros(block.shape, dtype)
    return jnp.where(mask_ref[i * width + k : i * width + k + 1, :] > 0, block, 0.0).astype(dtype)


def near_kernel(
    far, held_ref, mask_ref, first_ref, before_ref, *refs
):
    mid_refs = refs[: REACH - HEAD - far]
    (
        panel_ref, stay_ref, leave_ref, part_ref, high_ref, cube_ref, square, result, columns_ref, sem,
    ) = refs[REACH - HEAD - far :]
    reach = REACH
    lead = reach - HEAD
    scalars = pltpu.make_async_copy(held_ref, columns_ref, sem)
    scalars.start()
    half, size = stay_ref.shape[1], stay_ref.shape[2]
    width = panel_ref.shape[0] // size
    near = reach - far
    low_cols = reach + far
    far_cols = 2 * reach + far
    near_cols = 2 * reach
    for q, mid_ref in zip(range(far, lead), mid_refs):
        for k in range(reach + 1 + q):
            panel_ref[blocks(q, q + 1, size), blocks(k, k + 1, size)] = mid_ref[k]
    result[:, blocks(width, width + 1, size)] = jnp.zeros((near * size, size), result.dtype)
    left = panel_ref[blocks(reach, 2 * reach, size), blocks(far, lead, size)]
    for p in range(width // 2):
        cols = blocks(2 * p, 2 * p + 2, size)
        value = first_ref[:, cols]
        if 2 * p < near_cols:
            value = value + jnp.dot(
                left, panel_ref[blocks(far, lead, size), cols], preferred_element_type=jnp.float32
            )
        for i in range(reach):
            for k in (2 * p, 2 * p + 1):
                block = value[blocks(i, i + 1, size), blocks(k - 2 * p, k - 2 * p + 1, size)]
                here = (blocks(i, i + 1, size), blocks(k, k + 1, size))
                if i < far and k < low_cols:
                    part_ref[here] = block
                    square[here] = jnp.zeros((size, size), square.dtype)
                else:
                    square[here] = keep_block(mask_ref, i, k, width, block, square.dtype)
    rest = slice(far * size, reach * size)
    for p in range(width // 2):
        cols = blocks(2 * p, 2 * p + 2, size)
        low = max(far, 2 * p - reach)
        high = min(width, 2 * p + 2 + reach)
        value = jnp.dot(
            square[rest, blocks(low, high, size)],
            panel_ref[blocks(low, high, size), cols],
            preferred_element_type=jnp.float32,
        )
        result[:, cols] = (3.0 * square[rest, cols].astype(jnp.float32) - 2.0 * value).astype(result.dtype)
        low = max(low_cols, 2 * p - reach)
        high = min(far_cols, 2 * p + 2 + reach)
        if 2 * p < far_cols:
            if low < high:
                cube_ref[:, cols] = jnp.dot(
                    square[: far * size, blocks(low, high, size)],
                    panel_ref[blocks(low, high, size), cols],
                    preferred_element_type=jnp.float32,
                )
            else:
                cube_ref[:, cols] = jnp.zeros((far * size, 2 * size), jnp.float32)
    high_ref[...] = square[: far * size, blocks(low_cols, far_cols, size)]
    scalars.wait()
    for i in range(near):
        index = jnp.where(lax.axis_index("col") == 0, i, near - 1 - i)
        for s in range(2 * half):
            place = pl.multiple_of(own_place(columns_ref, i + reach + far, s, width) * size, size)
            target = stay_ref if s < half else leave_ref
            target[index, s % half] = result[blocks(i, i + 1, size), pl.ds(place, size)]


def far_kernel(
    far, i, mask_ref, spot_ref, part_ref, high_ref, cube_ref, row_ref, after_ref, before_ref,
    panel_ref, stay_ref, leave_ref, square, scratch
):
    reach = REACH
    result = scratch if i else stay_ref
    half, size = leave_ref.shape[1], leave_ref.shape[2]
    width = panel_ref.shape[0] // size
    low_cols = reach + far
    far_cols = 2 * reach + far
    mine = blocks(i, i + 1, size)
    for k in range(reach + 1 + i):
        panel_ref[mine, blocks(k, k + 1, size)] = row_ref[k]
    left = panel_ref[blocks(reach + i, reach + i + 1, size), blocks(0, far, size)]
    for p in range(low_cols // 2):
        cols = blocks(2 * p, 2 * p + 2, size)
        value = part_ref[mine, cols] + jnp.dot(
            left, panel_ref[blocks(0, far, size), cols], preferred_element_type=jnp.float32
        )
        for k in (2 * p, 2 * p + 1):
            block = value[:, blocks(k - 2 * p, k - 2 * p + 1, size)]
            square[:, blocks(k, k + 1, size)] = keep_block(mask_ref, i, k, width, block, square.dtype)
    for p in range(far_cols // 2):
        cols = blocks(2 * p, 2 * p + 2, size)
        low = max(0, 2 * p - reach)
        value = cube_ref[mine, cols] + jnp.dot(
            square[:, blocks(low, low_cols, size)],
            panel_ref[blocks(low, low_cols, size), cols],
            preferred_element_type=jnp.float32,
        )
        if 2 * p < low_cols:
            kept = square[:, cols]
        else:
            kept = high_ref[mine, blocks(2 * p - low_cols, 2 * p + 2 - low_cols, size)]
        result[:, cols] = (3.0 * kept.astype(jnp.float32) - 2.0 * value).astype(result.dtype)
    for s in range(0 if i else half, 2 * half):
        target = stay_ref if s < half else leave_ref
        target[0, s % half] = chosen(result, spot_ref, i, s, 2 * half)


def chosen(result, spot_ref, i, s, slots):
    size = result.shape[0]
    window = 2 * REACH + 1
    block = jnp.zeros((size, size), result.dtype)
    for d in range(window):
        if d == REACH and s % (slots // 2):
            continue
        at = (i * slots + s) * window + d
        block = jnp.where(spot_ref[at : at + 1, :] > 0, result[:, blocks(i + d, i + d + 1, size)], block)
    return block


def start_rows(pieces, out_ref, sems, first=0):
    straight = lax.axis_index("col") == 0
    copies = []
    for rows_ref, here, there in pieces:
        for n in range(rows_ref.shape[0]):
            to = out_ref.at[jnp.where(straight, here, there) + n]
            copies.append(pltpu.make_async_copy(rows_ref.at[n], to, sems.at[first + len(copies)]))
    for copy in copies:
        copy.start()
    return copies


def write_rows(pieces, out_ref, sems):
    for copy in start_rows(pieces, out_ref, sems):
        copy.wait()


def store_near_kernel(near_ref, out_ref, mark_ref, sems):
    rows, near = out_ref.shape[0], near_ref.shape[0]
    write_rows(((near_ref, rows // 2 - near, rows // 2),), out_ref, sems)
    mark_ref[...] = jnp.zeros_like(mark_ref)


def store_kernel(result_ref, spot_ref, got_near_ref, *refs):
    *row_refs, before_ref, out_ref, stay, sems = refs
    rows, near, half = out_ref.shape[0], got_near_ref.shape[0], out_ref.shape[1]
    count = len(row_refs) // 2
    pieces = [(got_near_ref, rows - 1 - count - near, 1 + count)]
    pieces += [(ref, 1 + i, rows - 2 - i) for i, ref in enumerate(row_refs[:count])]
    pieces += [(ref, rows - 2 - i, 1 + i) for i, ref in enumerate(row_refs[count:])]
    copies = start_rows(pieces, out_ref, sems)
    for s in range(half):
        stay[0, s] = chosen(result_ref, spot_ref, 0, s, 2 * half)
    copies += start_rows(((stay, 0, rows - 1),), out_ref, sems, len(copies))
    for copy in copies:
        copy.wait()


def finish_kernel(got_ref, before_ref, out_ref, sems):
    write_rows(((got_ref, out_ref.shape[0] - got_ref.shape[0], 0),), out_ref, sems)


def local(matrix, columns):
    local_rows, own_slots, size = matrix.shape[:3]
    dtype = matrix.dtype
    reach = REACH
    far = reach // 2
    near = reach - far
    cols = lax.axis_size("col")
    ring = lax.axis_size("row")
    width = local_rows + reach
    low_cols = reach + far
    far_cols = 2 * reach + far
    same = [(r * cols, (r + 1) % ring * cols) for r in range(ring)] + [
        (r * cols + 1, (r - 1) % ring * cols + 1) for r in range(ring)
    ]
    swap = [(r * cols + 1, (r + 1) % ring * cols) for r in range(ring)] + [
        (r * cols, (r - 1) % ring * cols + 1) for r in range(ring)
    ]
    beside = [(i, (i + 1) % cols) for i in range(cols)]
    axes = ("row", "col")
    edge_rows = own_slots * size
    in_place = pltpu.with_memory_space_constraint(matrix, pltpu.HBM)
    same_edge, swap_edge, held = pl.pallas_call(
        functools.partial(edge_kernel, HEAD),
        out_shape=(
            jax.ShapeDtypeStruct((edge_rows + TILE, size), dtype),
            jax.ShapeDtypeStruct((edge_rows, size), dtype),
            jax.ShapeDtypeStruct(columns.shape, columns.dtype),
        ),
        in_specs=[HBM, HBM],
        out_specs=(VMEM,) * 3,
        scratch_shapes=[pltpu.VMEM((TILE, size), jnp.float32), pltpu.SemaphoreType.DMA((3,))],
        compiler_params=limit(1),
        cost_estimate=LIGHT,
        name="edge",
    )(pltpu.with_memory_space_constraint(columns, pltpu.HBM), in_place)
    same_rows = lax.ppermute(same_edge, axes, same)
    swap_rows = lax.ppermute(swap_edge, axes, swap)
    sent, held = lax.optimization_barrier((matrix, held))
    other = lax.ppermute(sent, "col", beside)

    lead = reach - HEAD
    scalars = pltpu.SMEM(columns.shape, columns.dtype)
    panel_shape = jax.ShapeDtypeStruct((width * size, (width + 1) * size), dtype)
    first_shape = jax.ShapeDtypeStruct((reach * size, width * size), jnp.float32)
    base_shapes = (
        panel_shape,
        first_shape,
        jax.ShapeDtypeStruct((reach * width, size), jnp.float32),
        jax.ShapeDtypeStruct((far * 2 * own_slots * (2 * reach + 1), size), jnp.float32),
    )

    def base(turn, *before):
        return pl.pallas_call(
            functools.partial(base_kernel, turn),
            out_shape=base_shapes,
            in_specs=[VMEM, HBM, VMEM] + [VMEM] * len(before),
            out_specs=(VMEM,) * 4,
            input_output_aliases={3 + n: n for n in range(len(before))},
            scratch_shapes=[
                pltpu.VMEM(matrix.shape, dtype),
                scalars,
                pltpu.SMEM((reach, width + 1), jnp.int32),
                pltpu.SemaphoreType.DMA((2,)),
            ],
            compiler_params=limit(12),
            cost_estimate=LIGHT,
            name="base",
        )(held, in_place, other, *before)

    early = base(0)
    packed = pl.pallas_call(
        pack_kernel,
        out_shape=tuple(
            jax.ShapeDtypeStruct((reach + 1 + f, size, size), dtype) for f in range(lead)
        ),
        in_specs=[VMEM, HBM, VMEM, ANY],
        out_specs=(VMEM,) * lead,
        scratch_shapes=[
            pltpu.VMEM((lead,) + matrix.shape[1:], dtype),
            scalars,
            pltpu.SemaphoreType.DMA((2,)),
        ],
        compiler_params=limit(2),
        cost_estimate=LIGHT,
        name="pack",
    )(held, in_place, other, early[2])
    arrived = {f: lax.ppermute(packed[f], axes, swap) for f in reversed(range(lead))}

    panel, first_part, mask, spot = base(1, *early)
    panel, first_part = pl.pallas_call(
        functools.partial(lead_kernel, own_slots),
        out_shape=(panel_shape, first_shape),
        in_specs=[VMEM] * 4,
        out_specs=(VMEM,) * 2,
        input_output_aliases={2: 0, 3: 1},
        scratch_shapes=[
            pltpu.VMEM((TILE, size), jnp.int32),
            pltpu.SMEM((TILE, size), jnp.int32),
            pltpu.SemaphoreType.DMA,
        ],
        compiler_params=limit(12),
        cost_estimate=MEDIUM,
        name="lead",
    )(same_rows, swap_rows, panel, first_part)

    rows_out = jax.ShapeDtypeStruct((near, own_slots, size, size), dtype)
    panel, stay_near, leave_near, part, high, cube = pl.pallas_call(
        functools.partial(near_kernel, far),
        out_shape=(
            panel_shape,
            rows_out,
            rows_out,
            jax.ShapeDtypeStruct((far * size, low_cols * size), jnp.float32),
            jax.ShapeDtypeStruct((far * size, (far_cols - low_cols) * size), dtype),
            jax.ShapeDtypeStruct((far * size, far_cols * size), jnp.float32),
        ),
        in_specs=[VMEM] * (4 + lead - far),
        out_specs=(VMEM,) * 6,
        input_output_aliases={3: 0},
        scratch_shapes=[
            pltpu.VMEM((reach * size, width * size), dtype),
            pltpu.VMEM((near * size, (width + 1) * size), dtype),
            scalars,
            pltpu.SemaphoreType.DMA,
        ],
        compiler_params=limit(16),
        cost_estimate=SHORT,
        name="near",
    )(held, mask, first_part, panel, *[arrived[f] for f in range(far, lead)])
    arrived_near = lax.ppermute(leave_near, "col", beside)

    out, mark = pl.pallas_call(
        store_near_kernel,
        out_shape=(jax.ShapeDtypeStruct(matrix.shape, dtype), jax.ShapeDtypeStruct((8, size), jnp.float32)),
        in_specs=[VMEM],
        out_specs=(HBM, VMEM),
        scratch_shapes=[pltpu.SemaphoreType.DMA((near,))],
        compiler_params=limit(1),
        cost_estimate=LIGHT,
        name="store_near",
    )(stay_near)
    row_out = jax.ShapeDtypeStruct((1, own_slots, size, size), dtype)
    result_out = jax.ShapeDtypeStruct((size, far_cols * size), dtype)
    stay, got = {}, {}
    for i in reversed(range(far)):
        panel, stay[i], leave = pl.pallas_call(
            functools.partial(far_kernel, far, i),
            out_shape=(panel_shape, row_out if i else result_out, row_out),
            in_specs=[VMEM] * 8,
            out_specs=(VMEM,) * 3,
            input_output_aliases={7: 0},
            scratch_shapes=[
                pltpu.VMEM((size, low_cols * size), dtype),
                pltpu.VMEM((size, far_cols * size), dtype),
            ],
            compiler_params=limit(16),
            cost_estimate=HEAVY if i else LIGHT,
            name="far",
        )(mask, spot, part, high, cube, arrived[i], mark, panel)
        got[i] = lax.ppermute(leave, "col", beside)
    rest = range(1, far)
    pieces = [stay[0], spot, arrived_near, *[stay[i] for i in rest], *[got[i] for i in rest]]
    out = pl.pallas_call(
        store_kernel,
        out_shape=jax.ShapeDtypeStruct(matrix.shape, dtype),
        in_specs=[VMEM] * len(pieces) + [HBM],
        out_specs=HBM,
        input_output_aliases={len(pieces): 0},
        scratch_shapes=[
            pltpu.VMEM((1,) + matrix.shape[1:], dtype),
            pltpu.SemaphoreType.DMA((local_rows - near - 1,)),
        ],
        compiler_params=limit(2),
        cost_estimate=LIGHT,
        name="store",
    )(*pieces, out)
    return pl.pallas_call(
        finish_kernel,
        out_shape=jax.ShapeDtypeStruct(matrix.shape, dtype),
        in_specs=[VMEM, HBM],
        out_specs=HBM,
        input_output_aliases={1: 0},
        scratch_shapes=[pltpu.SemaphoreType.DMA((1,))],
        compiler_params=limit(1),
        cost_estimate=LIGHT,
        name="finish",
    )(got[0], out)


def solution(mesh):
    placed = (P(("geom", "row"), "col", None, None), P("row", None))
    return jax.shard_map(
        local,
        mesh=mesh,
        in_specs=placed,
        out_specs=P(("geom", "row"), "col", None, None),
        check_vma=False,
    )
```
